32 devices in a mesh: seg: 4 (over x, core), tr: 8 (over z, y).
Axes of the slice: x: 2, y: 2, z: 4, core: 2. Of those that a mesh axis runs over, the one named last changes fastest.
Arguments:
- energies: float32 [1], replicated, may hold values from -0.1 to 0.1
- hamiltonian: bfloat16 [8, 768, 768], P('seg'), may hold values from -4 to 4
- coupling: bfloat16 [8, 768, 768], P('seg'), may hold values from -1.5 to 1.5
- seed_inverse: bfloat16 [2, 1, 8, 768, 768], P(None, None, 'seg'), may hold values from -2 to 2
- lead_green: bfloat16 [2, 1, 768, 768], P(None, None, None, 'tr'), may hold values from -1 to 1
Outputs:
- green: bfloat16 [2, 1, 8, 768, 768], P(None, None, 'seg', None, 'tr')
The draws below stay inside these ranges and needn't reach their ends.
All inputs are finite; a program needn't handle non-finite values.
Results may differ from the reference program's by a relative error of at most 0.025.
Values may be sent and summed in bfloat16 or wider, within the bound.
A program may use at most 64 MiB of HBM per device.

```python
import jax
import jax.numpy as jnp

B = 768
ENERGIES = 1
SLABS = 8


broadening = 0.6


def level_values(key):
    return jax.random.uniform(jax.random.fold_in(key, 101), (SLABS, B), jnp.float32, -1.4, 1.4)


def hopping_values(key):
    raw = jax.random.normal(jax.random.fold_in(key, 102), (SLABS, B, B), jnp.float32)
    symmetric = (raw + jnp.swapaxes(raw, 1, 2)) * (0.25 / jnp.sqrt(2.0 * B))
    return symmetric * (1.0 - jnp.eye(B, dtype=jnp.float32))[None]


def energy_values(key):
    return jax.random.uniform(jax.random.fold_in(key, 103), (ENERGIES,), jnp.float32, -0.1, 0.1)


def draw_energies(key, part):
    return energy_values(key)


def draw_hamiltonian(key, part):
    levels = level_values(key)
    identity = jnp.eye(B, dtype=jnp.float32)
    return (hopping_values(key) + identity[None] * levels[:, :, None]).astype(jnp.bfloat16)


def draw_coupling(key, part):
    levels = level_values(key)
    strength = jnp.sqrt(0.8 * (levels * levels + broadening * broadening))
    raw = jnp.clip(jax.random.normal(jax.random.fold_in(key, 105), (SLABS, B, B), jnp.float32), -3.5, 3.5)
    noise = raw * (0.22 / jnp.sqrt(1.0 * B))
    identity = jnp.eye(B, dtype=jnp.float32)
    return (noise + identity[None] * strength[:, :, None]).astype(jnp.bfloat16)


def draw_seed_inverse(key, part):
    levels = level_values(key)
    hopping = hopping_values(key)
    energy = energy_values(key)
    offset = energy[:, None, None] - levels[None]
    denom = offset * offset + broadening * broadening
    inv_real = offset / denom
    inv_imag = -broadening / denom
    outer_real = inv_real[:, :, :, None] * inv_real[:, :, None, :] - inv_imag[:, :, :, None] * inv_imag[:, :, None, :]
    outer_imag = inv_real[:, :, :, None] * inv_imag[:, :, None, :] + inv_imag[:, :, :, None] * inv_real[:, :, None, :]
    identity = jnp.eye(B, dtype=jnp.float32)
    seed_real = identity * inv_real[:, :, :, None] - hopping[None] * outer_real
    seed_imag = identity * inv_imag[:, :, :, None] - hopping[None] * outer_imag
    return jnp.stack([seed_real, seed_imag]).astype(jnp.bfloat16)


def draw_lead_green(key, part):
    identity = jnp.eye(B, dtype=jnp.float32)
    diag_real = jax.random.uniform(jax.random.fold_in(key, 106), (ENERGIES, B), jnp.float32, -0.4, 0.4)
    diag_imag = jax.random.uniform(jax.random.fold_in(key, 107), (ENERGIES, B), jnp.float32, -0.8, -0.2)
    noise = jax.random.normal(jax.random.fold_in(key, 108), (2, ENERGIES, B, B), jnp.float32) * (0.3 / jnp.sqrt(1.0 * B))
    diagonal = jnp.stack([diag_real, diag_imag])[:, :, :, None] * identity
    return (noise + diagonal).astype(jnp.bfloat16)


def setup_inputs(seed: int = 0) -> dict:
    arg_keys = jax.random.split(jax.random.key(seed), 6)
    energies = draw_energies(jax.random.fold_in(arg_keys[5], 71), 0)
    hamiltonian = draw_hamiltonian(jax.random.fold_in(arg_keys[5], 71), 0)
    coupling = draw_coupling(jax.random.fold_in(arg_keys[5], 71), 0)
    seed_inverse = draw_seed_inverse(jax.random.fold_in(arg_keys[5], 71), 0)
    lead_green = draw_lead_green(jax.random.fold_in(arg_keys[5], 71), 0)
    return dict(energies=energies, hamiltonian=hamiltonian, coupling=coupling, seed_inverse=seed_inverse, lead_green=lead_green)


broadening = 0.6


def product(left, right):
    return jnp.dot(left, right, preferred_element_type=jnp.float32)


def pair_product(left_real, left_imag, right_real, right_imag):
    real_part = product(left_real, right_real) - product(left_imag, right_imag)
    imag_part = product(left_real, right_imag) + product(left_imag, right_real)
    return real_part, imag_part


def slab_step(energy, onsite, couple, seed_real, seed_imag, before_real, before_imag):
    weight_real = product(couple.T, seed_real).astype(jnp.bfloat16)
    weight_imag = product(couple.T, seed_imag).astype(jnp.bfloat16)
    summed_real, summed_imag = pair_product(before_real, before_imag, weight_real, weight_imag)
    carry_real = summed_real.astype(jnp.bfloat16)
    carry_imag = summed_imag.astype(jnp.bfloat16)
    seed_real32 = seed_real.astype(jnp.float32)
    seed_imag32 = seed_imag.astype(jnp.float32)
    probe_real = energy * seed_real32 - broadening * seed_imag32 - product(onsite, seed_real) - product(couple, carry_real)
    probe_imag = energy * seed_imag32 + broadening * seed_real32 - product(onsite, seed_imag) - product(couple, carry_imag)
    probe_real = probe_real.astype(jnp.bfloat16)
    probe_imag = probe_imag.astype(jnp.bfloat16)
    back_real, back_imag = pair_product(seed_real, seed_imag, probe_real, probe_imag)
    green_real = (2.0 * seed_real32 - back_real).astype(jnp.bfloat16)
    green_imag = (2.0 * seed_imag32 - back_imag).astype(jnp.bfloat16)
    return green_real, green_imag


def reference(energies, hamiltonian, coupling, seed_inverse, lead_green):
    results = []
    for energy_index in range(ENERGIES):
        before_real = lead_green[0, energy_index]
        before_imag = lead_green[1, energy_index]
        chain_blocks = []
        for slab_index in range(SLABS):
            before_real, before_imag = slab_step(energies[energy_index], hamiltonian[slab_index], coupling[slab_index], seed_inverse[0, energy_index, slab_index], seed_inverse[1, energy_index, slab_index], before_real, before_imag)
            chain_blocks.append(jnp.stack([before_real, before_imag]))
        results.append(jnp.stack(chain_blocks, axis=1))
    return jnp.stack(results, axis=1)
```

```python
import functools

import jax
import jax.numpy as jnp
from jax import lax
from jax.experimental import pallas as pl
from jax.experimental.pallas import tpu as pltpu
from jax.sharding import PartitionSpec as P

broadening = 0.6
LANES = 128


def mm(left, right):
    return jnp.dot(left, right, preferred_element_type=jnp.float32)


def pick(index, values):
    total = jnp.int32(0)
    for place, value in enumerate(values):
        total = total + jnp.where(index == place, jnp.int32(value), jnp.int32(0))
    return total


def kernel(
    nseg, n, width, pad,
    energies, ham, cpl, seed, lead, out,
    ct, gath, mix, vec, uvec, bias, acc, car,
    vs_sem, vr_sem, cs_sem, cr_sem, gs_sem, gr_sem, fs_sem, fr_sem, bs_sem, br_sem,
):
    slabs = ham.shape[0]
    order = ham.shape[1]
    half = order // 2
    steps = n // 2
    ticks = 2 * steps
    wide = 2 * pad
    chains = 2 * slabs
    seg = lax.axis_index("seg")
    tr = lax.axis_index("tr")
    role = seg % 2
    low = role == 0
    high = role == 1
    first = seg == 0
    partner = seg + 1 - 2 * role
    linked = jnp.logical_and(high, seg + 1 < nseg)
    fed = jnp.logical_and(low, seg > 0)

    def place_of(t):
        odd = t % 2
        return odd * (n - 1 - t // 2) + (1 - odd) * (t // 2)

    def tr_at(position):
        position = (position + 2 * n) % n
        past = position // steps
        return (1 - past) * (2 * position) + past * (2 * (n - 1 - position) + 1)

    me = place_of(tr)
    following, preceding = tr_at(me + 1), tr_at(me - 1)

    barrier = pltpu.get_barrier_semaphore()

    def greet(s, t):
        pl.semaphore_signal(
            barrier, inc=1, device_id=(s, t), device_id_type=pl.DeviceIdType.MESH
        )

    greet(partner, tr)

    @pl.when(low)
    def _():
        greet(seg, following)
        greet(seg, preceding)

    @pl.when(fed)
    def _():
        greet(seg - 1, tr)

    @pl.when(linked)
    def _():
        greet(seg + 1, tr)

    peers = 1 + 2 * (1 - role) + jnp.where(jnp.logical_or(fed, linked), 1, 0)
    pl.semaphore_wait(barrier, peers)

    def remote(src, dst, send, recv, s, t):
        return pltpu.make_async_remote_copy(
            src_ref=src, dst_ref=dst, send_sem=send, recv_sem=recv,
            device_id=(s, t), device_id_type=pl.DeviceIdType.MESH,
        )

    def ring_next(s, h):
        owner = tr_at(me - s)
        return remote(
            gath.at[owner, h], gath.at[owner, h], fs_sem.at[s, h], fr_sem.at[s, h], seg, following
        )

    def ring_prev(s, h):
        owner = tr_at(me + s)
        return remote(
            gath.at[owner, h], gath.at[owner, h], bs_sem.at[s, h], br_sem.at[s, h], seg, preceding
        )

    def goes_next(s, h):
        return jnp.logical_or(s < steps - 1, h == 0)

    def goes_prev(s, h):
        return jnp.logical_or(s < steps - 1, h == 1)

    def ring_start(s, h):
        @pl.when(goes_next(s, h))
        def _():
            ring_next(s, h).start()

        @pl.when(goes_prev(s, h))
        def _():
            ring_prev(s, h).start()

    def tick(j):
        s, h = j // 2, j % 2

        @pl.when(goes_next(s, h))
        def _():
            ring_next(s, h).wait_recv()

        @pl.when(goes_prev(s, h))
        def _():
            ring_prev(s, h).wait_recv()

        @pl.when(s + 1 < steps)
        def _():
            ring_start(s + 1, h)

    def send_vec(k):
        return remote(
            vec.at[k], vec.at[slabs + k], vs_sem.at[k], vr_sem.at[k], partner, tr
        )

    def send_car(k):
        return remote(
            car.at[slabs + k], car.at[k], cs_sem.at[k], cr_sem.at[k], partner, tr
        )

    def send_block(h, s):
        return remote(
            car.at[slabs - 1, pl.ds(h * half, half)], gath.at[tr, h],
            gs_sem.at[h], gr_sem.at[h], s, tr,
        )

    @pl.when(first)
    def _():
        for h in range(2):
            rows = slice(h * half, (h + 1) * half)
            gath[tr, h] = jnp.zeros((half, wide), jnp.bfloat16)
            gath[tr, h, :, 0:width] = lead[0, 0, rows, :]
            gath[tr, h, :, pad : pad + width] = lead[1, 0, rows, :]
            ring_start(0, h)

    row = lax.broadcasted_iota(jnp.int32, (order, wide), 0)
    lane = lax.broadcasted_iota(jnp.int32, (order, wide), 1)
    chosen = jnp.logical_and(row == tr * width + lane, lane < width)
    unit = jnp.where(chosen, 1.0, 0.0).astype(jnp.bfloat16)
    for k in range(slabs):
        vec[k] = unit
        ct[k] = jnp.transpose(cpl[k])

    energy = energies[0]

    def times_seed(b, value):
        by_real = mm(seed[0, 0, b], value)
        by_imag = mm(seed[1, 0, b], value)
        real = by_real[:, :pad] - by_imag[:, pad:]
        imag = by_real[:, pad:] + by_imag[:, :pad]
        return jnp.concatenate([real, imag], axis=1)

    own_back = [(k, b) for k in reversed(range(slabs)) for b in reversed(range(k + 1))]
    far = [(slabs + k, b) for k in reversed(range(slabs)) for b in reversed(range(slabs))]
    back = own_back + far
    own_count, far_count = len(own_back), len(far)

    def back_pass(i, carry):
        k = pick(i, [item[0] for item in back])
        b = pick(i, [item[1] for item in back])
        for index, (chain, slab) in enumerate(far):
            if slab == slabs - 1:
                @pl.when(i == own_count + index)
                def _(chain=chain):
                    send_vec(chain - slabs).wait_recv()

        u = times_seed(b, vec[k]).astype(jnp.bfloat16)
        uvec[k, b] = u
        onsite = mm(ham[b], u)
        vec[k] = mm(ct[b], u).astype(jnp.bfloat16)
        u32 = u.astype(jnp.float32)
        real, imag = u32[:, :pad], u32[:, pad:]
        turned = jnp.concatenate([-imag, real], axis=1)
        bias[k, b] = energy * u32 + broadening * turned - onsite
        for index, (chain, slab) in enumerate(own_back):
            if slab == 0:
                @pl.when(jnp.logical_and(high, i == index))
                def _(chain=chain):
                    send_vec(chain).start()

        @pl.when(jnp.logical_and(first, i < ticks))
        def _():
            tick(i)

        return carry

    lax.fori_loop(0, own_count + (1 - role) * far_count, back_pass, 0)

    @pl.when(first)
    def _():
        def rest(j, carry):
            tick(j)
            return carry

        lax.fori_loop(min(own_count + far_count, ticks), ticks, rest, 0)

    @pl.when(low)
    def _():
        def build(t, carry):
            mix[t] = jnp.zeros((wide, chains * wide), jnp.bfloat16)
            rows = pl.ds(pl.multiple_of(t * width, 16), width)
            for k in range(chains):
                block = vec[k, rows, :]
                real, imag = block[:, :pad], block[:, pad:]
                base = k * wide
                mix[t, 0:width, base : base + wide] = block
                mix[t, pad : pad + width, base : base + pad] = -imag
                mix[t, pad : pad + width, base + pad : base + wide] = real
            return carry

        lax.fori_loop(0, n, build, 0)

        for h in range(2):
            @pl.when(fed)
            def _(h=h):
                send_block(h, seg).wait_recv()
                ring_start(0, h)

        for h in range(2):
            acc[h] = mm(gath[tr, h], mix[tr])

        def add(owner, h):
            acc[h] = acc[h] + mm(gath[owner, h], mix[owner])

        def arrive(j, carry):
            @pl.when(fed)
            def _():
                tick(j)

            s, h = j // 2, j % 2

            @pl.when(goes_next(s, h))
            def _():
                add(tr_at(me - 1 - s), h)

            @pl.when(goes_prev(s, h))
            def _():
                add(tr_at(me + 1 + s), h)

            return carry

        lax.fori_loop(0, ticks, arrive, 0)
        for k in range(chains):
            for h in range(2):
                car[k, h * half : (h + 1) * half, :] = acc[
                    h, :, k * wide : (k + 1) * wide
                ].astype(jnp.bfloat16)

    far_on = [(slabs + k, b) for k in reversed(range(slabs)) for b in range(slabs)]
    own_on = [(k, b) for k in reversed(range(slabs)) for b in range(k + 1)]
    onward = far_on + own_on

    def on_pass(i, carry):
        k = pick(i, [item[0] for item in onward])
        b = pick(i, [item[1] for item in onward])
        for index, (chain, slab) in enumerate(own_on):
            if slab == 0:
                @pl.when(jnp.logical_and(high, i == far_count + index))
                def _(chain=chain):
                    send_car(chain).wait_recv()

        probe = (bias[k, b] - mm(cpl[b], car[k])).astype(jnp.bfloat16)
        green = 2.0 * uvec[k, b].astype(jnp.float32) - times_seed(b, probe)
        car[k] = green.astype(jnp.bfloat16)
        for index, (chain, slab) in enumerate(far_on):
            if slab == slabs - 1:
                @pl.when(jnp.logical_and(low, i == index))
                def _(chain=chain):
                    send_car(chain - slabs).start()

        for index, (chain, slab) in enumerate(own_on):
            if slab == chain:
                @pl.when(i == far_count + index)
                def _(chain=chain):
                    if chain == slabs - 1:
                        @pl.when(linked)
                        def _():
                            for h in range(2):
                                send_block(h, seg + 1).start()

                    out[0, 0, chain] = car[chain, :, 0:width]
                    out[1, 0, chain] = car[chain, :, pad : pad + width]

        return carry

    lax.fori_loop(role * far_count, far_count + own_count, on_pass, 0)

    @pl.when(high)
    def _():
        for k in range(slabs):
            send_vec(k).wait_send()

    @pl.when(linked)
    def _():
        for h in range(2):
            send_block(h, seg + 1).wait_send()

    @pl.when(low)
    def _():
        for k in range(slabs):
            send_car(k).wait_send()

        def sent(j, carry):
            s, h = j // 2, j % 2

            @pl.when(goes_next(s, h))
            def _():
                ring_next(s, h).wait_send()

            @pl.when(goes_prev(s, h))
            def _():
                ring_prev(s, h).wait_send()

            return carry

        lax.fori_loop(0, ticks, sent, 0)


def local(nseg, n, energies, hamiltonian, coupling, seed_inverse, lead_green):
    slabs, order, _ = hamiltonian.shape
    width = lead_green.shape[3]
    pad = -(-width // LANES) * LANES
    wide = 2 * pad
    chains = 2 * slabs
    steps = n // 2
    vmem = pl.BlockSpec(memory_space=pltpu.VMEM)
    dma = pltpu.SemaphoreType.DMA
    bf16, f32 = jnp.bfloat16, jnp.float32
    return pl.pallas_call(
        functools.partial(kernel, nseg, n, width, pad),
        out_shape=jax.ShapeDtypeStruct((2, 1, slabs, order, width), bf16),
        in_specs=[pl.BlockSpec(memory_space=pltpu.SMEM)] + [vmem] * 4,
        out_specs=vmem,
        scratch_shapes=[
            pltpu.VMEM((slabs, order, order), bf16),
            pltpu.VMEM((n, 2, order // 2, wide), bf16),
            pltpu.VMEM((n, wide, chains * wide), bf16),
            pltpu.VMEM((chains, order, wide), bf16),
            pltpu.VMEM((chains, slabs, order, wide), bf16),
            pltpu.VMEM((chains, slabs, order, wide), f32),
            pltpu.VMEM((2, order // 2, chains * wide), f32),
            pltpu.VMEM((chains, order, wide), bf16),
            dma((slabs,)), dma((slabs,)), dma((slabs,)), dma((slabs,)),
            dma((2,)), dma((2,)),
            dma((steps, 2)), dma((steps, 2)), dma((steps, 2)), dma((steps, 2)),
        ],
        compiler_params=pltpu.CompilerParams(
            collective_id=0, has_side_effects=True, vmem_limit_bytes=60 * 2**20
        ),
    )(energies, hamiltonian, coupling, seed_inverse, lead_green)


def solution(mesh):
    in_specs = (
        P(),
        P("seg", None, None),
        P("seg", None, None),
        P(None, None, "seg", None, None),
        P(None, None, None, "tr"),
    )
    out_specs = P(None, None, "seg", None, "tr")
    body = functools.partial(local, mesh.shape["seg"], mesh.shape["tr"])
    return jax.shard_map(body, mesh=mesh, in_specs=in_specs, out_specs=out_specs, check_vma=False)
```

```python
import functools

import jax
import jax.numpy as jnp
from jax import lax
from jax.experimental import pallas as pl
from jax.experimental.pallas import tpu as pltpu
from jax.sharding import PartitionSpec as P

broadening = 0.6
LANES = 128


def mm(left, right):
    return jnp.dot(left, right, preferred_element_type=jnp.float32)


def mm_left_turned(left, right):
    return lax.dot_general(
        left, right, (((0,), (0,)), ((), ())), preferred_element_type=jnp.float32
    )


def when(condition):
    if isinstance(condition, bool):
        return (lambda body: body()) if condition else (lambda body: None)
    return pl.when(condition)


def kernel(
    nseg, n, width, pad,
    energies, ham, cpl, seed, lead, out,
    hm, cp, sd, ct, gath, mix, vec, uvec, bias, acc, car, turned_out,
    in_sem, vs_sem, vr_sem, cs_sem, cr_sem, gs_sem, gr_sem, fs_sem, fr_sem, bs_sem, br_sem,
):
    slabs = ham.shape[0]
    order = ham.shape[1]
    half = order // 2
    steps = n // 2
    ticks = 2 * steps
    wide = 2 * pad
    chains = 2 * slabs
    top = chains - 1
    seg = lax.axis_index("seg")
    tr = lax.axis_index("tr")
    role = seg % 2
    low = role == 0
    high = role == 1
    first = seg == 0
    partner = seg + 1 - 2 * role
    linked = jnp.logical_and(high, seg + 1 < nseg)
    fed = jnp.logical_and(low, seg > 0)

    def inputs_of(b):
        pairs = (
            (seed.at[0, 0, b], sd.at[0, b]),
            (seed.at[1, 0, b], sd.at[1, b]),
            (cpl.at[b], cp.at[b]),
            (ham.at[b], hm.at[b]),
        )
        return [
            pltpu.make_async_copy(src, dst, in_sem.at[place, b])
            for place, (src, dst) in enumerate(pairs)
        ]

    for b in reversed(range(slabs)):
        for copy in inputs_of(b):
            copy.start()

    def place_of(t):
        odd = t % 2
        return odd * (n - 1 - t // 2) + (1 - odd) * (t // 2)

    def tr_at(position):
        position = (position + 2 * n) % n
        past = position // steps
        return (1 - past) * (2 * position) + past * (2 * (n - 1 - position) + 1)

    me = place_of(tr)
    following, preceding = tr_at(me + 1), tr_at(me - 1)

    barrier = pltpu.get_barrier_semaphore()

    def greet(s, t):
        pl.semaphore_signal(
            barrier, inc=1, device_id=(s, t), device_id_type=pl.DeviceIdType.MESH
        )

    greet(partner, tr)

    @pl.when(low)
    def _():
        greet(seg, following)
        greet(seg, preceding)

    @pl.when(fed)
    def _():
        greet(seg - 1, tr)

    @pl.when(linked)
    def _():
        greet(seg + 1, tr)

    peers = 1 + 2 * (1 - role) + jnp.where(jnp.logical_or(fed, linked), 1, 0)
    pl.semaphore_wait(barrier, peers)

    def remote(src, dst, send, recv, s, t):
        return pltpu.make_async_remote_copy(
            src_ref=src, dst_ref=dst, send_sem=send, recv_sem=recv,
            device_id=(s, t), device_id_type=pl.DeviceIdType.MESH,
        )

    def ring_next(s, h):
        owner = tr_at(me - s)
        return remote(
            gath.at[owner, h], gath.at[owner, h], fs_sem.at[s, h], fr_sem.at[s, h], seg, following
        )

    def ring_prev(s, h):
        owner = tr_at(me + s)
        return remote(
            gath.at[owner, h], gath.at[owner, h], bs_sem.at[s, h], br_sem.at[s, h], seg, preceding
        )

    def goes_next(s, h):
        return (s < steps - 1) | (h == 0)

    def goes_prev(s, h):
        return (s < steps - 1) | (h == 1)

    def ring_start(s, h):
        when(goes_next(s, h))(lambda: ring_next(s, h).start())
        when(goes_prev(s, h))(lambda: ring_prev(s, h).start())

    def tick(j):
        s, h = j // 2, j % 2
        when(goes_next(s, h))(lambda: ring_next(s, h).wait_recv())
        when(goes_prev(s, h))(lambda: ring_prev(s, h).wait_recv())
        when(s + 1 < steps)(lambda: ring_start(s + 1, h))

    def send_vec(k):
        return remote(
            vec.at[k], vec.at[slabs + k], vs_sem.at[k], vr_sem.at[k], partner, tr
        )

    def send_car(k):
        return remote(
            car.at[slabs + k], car.at[k], cs_sem.at[k], cr_sem.at[k], partner, tr
        )

    def send_block(h, s):
        return remote(turned_out.at[h], gath.at[tr, h], gs_sem.at[h], gr_sem.at[h], s, tr)

    @pl.when(first)
    def _():
        for h in range(2):
            for part in range(2):
                gath[tr, h, part * width : (part + 1) * width, :] = lead[
                    part, 0, :, h * half : (h + 1) * half
                ]
            ring_start(0, h)

    row = lax.broadcasted_iota(jnp.int32, (order, wide), 0)
    lane = lax.broadcasted_iota(jnp.int32, (order, wide), 1)
    chosen = jnp.logical_and(row == tr * width + lane, lane < width)
    unit = jnp.where(chosen, 1.0, 0.0).astype(jnp.bfloat16)
    for k in range(slabs):
        vec[k] = unit

    energy = energies[0]
    far = list(reversed(range(slabs, chains)))
    own = list(reversed(range(slabs)))

    def side_by_side(blocks):
        return blocks[0] if len(blocks) == 1 else jnp.concatenate(blocks, axis=1)

    def times_seed(b, value):
        by_real = mm(sd[0, b], value)
        by_imag = mm(sd[1, b], value)
        blocks = []
        for base in range(0, value.shape[1], wide):
            middle, end = base + pad, base + wide
            blocks.append(by_real[:, base:middle] - by_imag[:, middle:end])
            blocks.append(by_real[:, middle:end] + by_imag[:, base:middle])
        return side_by_side(blocks)

    def back_stage(ks, b, fresh=False, pause=lambda: None):
        if fresh:
            for copy in inputs_of(b):
                copy.wait()
            couple_turned = jnp.transpose(cp[b])
            ct[b] = couple_turned
        u = times_seed(b, side_by_side([vec[k] for k in ks])).astype(jnp.bfloat16)
        for place, k in enumerate(ks):
            uvec[k, b] = u[:, place * wide : (place + 1) * wide]
        pause()
        before = mm(ct[b], u).astype(jnp.bfloat16)
        onsite = mm(hm[b], u)
        for place, k in enumerate(ks):
            block = slice(place * wide, (place + 1) * wide)
            vec[k] = before[:, block]
            u32 = u[:, block].astype(jnp.float32)
            turned = jnp.concatenate([-u32[:, pad:], u32[:, :pad]], axis=1)
            bias[k, b] = energy * u32 + broadening * turned - onsite[:, block]
        pause()

    def back_loop(ks):
        def body(i, carry):
            back_stage(ks, slabs - 1 - i)
            return carry

        lax.fori_loop(0, slabs, body, 0)

    def on_stage(ks, b):
        value = side_by_side([car[k] for k in ks])
        bent = side_by_side([bias[k, b] for k in ks])
        probe = (bent - mm(cp[b], value)).astype(jnp.bfloat16)
        twice = 2.0 * side_by_side([uvec[k, b] for k in ks]).astype(jnp.float32)
        green = (twice - times_seed(b, probe)).astype(jnp.bfloat16)
        for place, k in enumerate(ks):
            car[k] = green[:, place * wide : (place + 1) * wide]

    def on_loop(ks, count):
        def body(b, carry):
            on_stage(ks, b)
            return carry

        lax.fori_loop(0, count, body, 0)

    def emit(k):
        block = car[k]
        parts = [
            jnp.transpose(block[:, base : base + pad])[:width] for base in (0, pad)
        ]
        if k == slabs - 1:
            @pl.when(linked)
            def _():
                for h in range(2):
                    for part in range(2):
                        turned_out[h, part * width : (part + 1) * width, :] = parts[part][
                            :, h * half : (h + 1) * half
                        ]
                    send_block(h, seg + 1).start()

        for part in range(2):
            out[part, 0, k] = parts[part]

    def build(ks):
        def body(t, carry):
            rows = pl.ds(pl.multiple_of(t * width, 16), width)
            for k in ks:
                block = vec[k, rows, :]
                base = k * wide
                mix[t, 0:width, base : base + wide] = block
                mix[t, width : 2 * width, base : base + pad] = -block[:, pad:]
                mix[t, width : 2 * width, base + pad : base + wide] = block[:, :pad]
            return carry

        lax.fori_loop(0, n, body, 0)

    def gathered_times(ks):
        start, stop = min(ks) * wide, (max(ks) + 1) * wide
        for h in range(2):
            total = mm_left_turned(gath[0, h], mix[0, :, start:stop])
            for t in range(1, n):
                total = total + mm_left_turned(gath[t, h], mix[t, :, start:stop])
            total = total.astype(jnp.bfloat16)
            for k in ks:
                car[k, h * half : (h + 1) * half, :] = total[
                    :, k * wide - start : (k + 1) * wide - start
                ]

    @pl.when(high)
    def _():
        for k in own:
            for b in reversed(range(k + 1)):
                back_stage([k], b, fresh=k == slabs - 1)
            send_vec(k).start()
        for k in own:
            send_car(k).wait_recv()
            on_loop([k], k + 1)
            emit(k)

    @pl.when(first)
    def _():
        waiting = list(range(ticks))

        def pause():
            if waiting:
                tick(waiting.pop(0))

        for b in own:
            back_stage(own[: slabs - b], b, fresh=True, pause=pause)
        send_vec(top - slabs).wait_recv()
        for b in own:
            back_stage([top], b, pause=pause)
        build([top])
        while waiting:
            pause()
        gathered_times([top])
        on_loop([top], slabs)
        send_car(top - slabs).start()
        for k in far[1:]:
            send_vec(k - slabs).wait_recv()
        back_loop(far[1:])
        build(far[1:] + own)
        gathered_times(far[1:] + own)
        on_loop(far[1:], slabs)
        for k in far[1:]:
            send_car(k - slabs).start()

    @pl.when(fed)
    def _():
        for b in own:
            back_stage(own[: slabs - b], b, fresh=True)
        for k in far:
            send_vec(k - slabs).wait_recv()
        back_loop(far)
        build(far + own)
        for h in range(2):
            send_block(h, seg).wait_recv()
            ring_start(0, h)
        for h in range(2):
            acc[h] = mm_left_turned(gath[tr, h], mix[tr])

        def add(owner, h):
            acc[h] = acc[h] + mm_left_turned(gath[owner, h], mix[owner])

        def arrive(j, carry):
            tick(j)
            s, h = j // 2, j % 2
            when(goes_next(s, h))(lambda: add(tr_at(me - 1 - s), h))
            when(goes_prev(s, h))(lambda: add(tr_at(me + 1 + s), h))
            return carry

        lax.fori_loop(0, ticks, arrive, 0)
        for k in range(chains):
            for h in range(2):
                car[k, h * half : (h + 1) * half, :] = acc[
                    h, :, k * wide : (k + 1) * wide
                ].astype(jnp.bfloat16)
        on_loop(far, slabs)
        for k in far:
            send_car(k - slabs).start()

    @pl.when(low)
    def _():
        for b in range(slabs):
            on_stage(own[: slabs - b], b)
            emit(b)

    @pl.when(high)
    def _():
        for k in range(slabs):
            send_vec(k).wait_send()

    @pl.when(linked)
    def _():
        for h in range(2):
            send_block(h, seg + 1).wait_send()

    @pl.when(low)
    def _():
        for k in range(slabs):
            send_car(k).wait_send()

        def sent(j, carry):
            s, h = j // 2, j % 2

            when(goes_next(s, h))(lambda: ring_next(s, h).wait_send())
            when(goes_prev(s, h))(lambda: ring_prev(s, h).wait_send())

            return carry

        lax.fori_loop(0, ticks, sent, 0)


def local(nseg, n, energies, hamiltonian, coupling, seed_inverse, lead_green):
    slabs, order, _ = hamiltonian.shape
    width = lead_green.shape[3]
    pad = -(-width // LANES) * LANES
    wide = 2 * pad
    chains = 2 * slabs
    steps = n // 2
    vmem = pl.BlockSpec(memory_space=pltpu.VMEM)
    anywhere = pl.BlockSpec(memory_space=pl.ANY)
    dma = pltpu.SemaphoreType.DMA
    bf16, f32 = jnp.bfloat16, jnp.float32
    turned = pl.pallas_call(
        functools.partial(kernel, nseg, n, width, pad),
        out_shape=jax.ShapeDtypeStruct((2, 1, slabs, width, order), bf16),
        in_specs=[pl.BlockSpec(memory_space=pltpu.SMEM)] + [anywhere] * 3 + [vmem],
        out_specs=vmem,
        scratch_shapes=[
            pltpu.VMEM((slabs, order, order), bf16),
            pltpu.VMEM((slabs, order, order), bf16),
            pltpu.VMEM((2, slabs, order, order), bf16),
            pltpu.VMEM((slabs, order, order), bf16),
            pltpu.VMEM((n, 2, 2 * width, order // 2), bf16),
            pltpu.VMEM((n, 2 * width, chains * wide), bf16),
            pltpu.VMEM((chains, order, wide), bf16),
            pltpu.VMEM((chains, slabs, order, wide), bf16),
            pltpu.VMEM((chains, slabs, order, wide), f32),
            pltpu.VMEM((2, order // 2, chains * wide), f32),
            pltpu.VMEM((chains, order, wide), bf16),
            pltpu.VMEM((2, 2 * width, order // 2), bf16),
            dma((4, slabs)),
            dma((slabs,)), dma((slabs,)), dma((slabs,)), dma((slabs,)),
            dma((2,)), dma((2,)),
            dma((steps, 2)), dma((steps, 2)), dma((steps, 2)), dma((steps, 2)),
        ],
        compiler_params=pltpu.CompilerParams(
            collective_id=0, has_side_effects=True, vmem_limit_bytes=60 * 2**20
        ),
    )(energies, hamiltonian, coupling, seed_inverse, jnp.swapaxes(lead_green, 2, 3))
    return jnp.swapaxes(turned, 3, 4)


def solution(mesh):
    in_specs = (
        P(),
        P("seg", None, None),
        P("seg", None, None),
        P(None, None, "seg", None, None),
        P(None, None, None, "tr"),
    )
    out_specs = P(None, None, "seg", None, "tr")
    body = functools.partial(local, mesh.shape["seg"], mesh.shape["tr"])
    return jax.shard_map(body, mesh=mesh, in_specs=in_specs, out_specs=out_specs, check_vma=False)
```

```python
import functools

import jax
import jax.numpy as jnp
from jax import lax
from jax.experimental import pallas as pl
from jax.experimental.pallas import tpu as pltpu
from jax.sharding import PartitionSpec as P

broadening = 0.6
LANES = 128


def mm(left, right):
    return jnp.dot(left, right, preferred_element_type=jnp.float32)


def mm_left_turned(left, right):
    return lax.dot_general(
        left, right, (((0,), (0,)), ((), ())), preferred_element_type=jnp.float32
    )


def when(condition):
    if isinstance(condition, bool):
        return (lambda body: body()) if condition else (lambda body: None)
    return pl.when(condition)


def kernel(
    nseg, n, width, pad,
    energies, ham, cpl, seed, lead, out,
    hm, cp, sd, ct, gath, mix, vec, uvec, bias, acc, car, turned_out, left, aff,
    in_sem, vs_sem, vr_sem, cs_sem, cr_sem, gs_sem, gr_sem, fs_sem, fr_sem, bs_sem, br_sem,
):
    slabs = ham.shape[0]
    order = ham.shape[1]
    half = order // 2
    steps = n // 2
    ticks = 2 * steps
    wide = 2 * pad
    chains = 2 * slabs
    top = chains - 1
    seg = lax.axis_index("seg")
    tr = lax.axis_index("tr")
    role = seg % 2
    low = role == 0
    high = role == 1
    first = seg == 0
    partner = seg + 1 - 2 * role
    linked = jnp.logical_and(high, seg + 1 < nseg)
    fed = jnp.logical_and(low, seg > 0)

    def inputs_of(b):
        pairs = (
            (seed.at[0, 0, b], sd.at[0, b]),
            (seed.at[1, 0, b], sd.at[1, b]),
            (cpl.at[b], cp.at[b]),
            (ham.at[b], hm.at[b]),
        )
        return [
            pltpu.make_async_copy(src, dst, in_sem.at[place, b])
            for place, (src, dst) in enumerate(pairs)
        ]

    for b in reversed(range(slabs)):
        for copy in inputs_of(b):
            copy.start()

    def place_of(t):
        odd = t % 2
        return odd * (n - 1 - t // 2) + (1 - odd) * (t // 2)

    def tr_at(position):
        position = (position + 2 * n) % n
        past = position // steps
        return (1 - past) * (2 * position) + past * (2 * (n - 1 - position) + 1)

    me = place_of(tr)
    following, preceding = tr_at(me + 1), tr_at(me - 1)

    barrier = pltpu.get_barrier_semaphore()

    def greet(s, t):
        pl.semaphore_signal(
            barrier, inc=1, device_id=(s, t), device_id_type=pl.DeviceIdType.MESH
        )

    greet(partner, tr)

    @pl.when(low)
    def _():
        greet(seg, following)
        greet(seg, preceding)

    @pl.when(fed)
    def _():
        greet(seg - 1, tr)

    @pl.when(linked)
    def _():
        greet(seg + 1, tr)

    peers = 1 + 2 * (1 - role) + jnp.where(jnp.logical_or(fed, linked), 1, 0)
    pl.semaphore_wait(barrier, peers)

    def remote(src, dst, send, recv, s, t):
        return pltpu.make_async_remote_copy(
            src_ref=src, dst_ref=dst, send_sem=send, recv_sem=recv,
            device_id=(s, t), device_id_type=pl.DeviceIdType.MESH,
        )

    def ring_next(s, h):
        owner = tr_at(me - s)
        return remote(
            gath.at[owner, h], gath.at[owner, h], fs_sem.at[s, h], fr_sem.at[s, h], seg, following
        )

    def ring_prev(s, h):
        owner = tr_at(me + s)
        return remote(
            gath.at[owner, h], gath.at[owner, h], bs_sem.at[s, h], br_sem.at[s, h], seg, preceding
        )

    def goes_next(s, h):
        return (s < steps - 1) | (h == 0)

    def goes_prev(s, h):
        return (s < steps - 1) | (h == 1)

    def ring_start(s, h):
        when(goes_next(s, h))(lambda: ring_next(s, h).start())
        when(goes_prev(s, h))(lambda: ring_prev(s, h).start())

    def tick(j):
        s, h = j // 2, j % 2
        when(goes_next(s, h))(lambda: ring_next(s, h).wait_recv())
        when(goes_prev(s, h))(lambda: ring_prev(s, h).wait_recv())
        when(s + 1 < steps)(lambda: ring_start(s + 1, h))

    def send_vec(k):
        return remote(
            vec.at[k], vec.at[slabs + k], vs_sem.at[k], vr_sem.at[k], partner, tr
        )

    def send_car(k):
        return remote(
            car.at[slabs + k], car.at[k], cs_sem.at[k], cr_sem.at[k], partner, tr
        )

    def send_block(h, s):
        return remote(turned_out.at[h], gath.at[tr, h], gs_sem.at[h], gr_sem.at[h], s, tr)

    @pl.when(first)
    def _():
        for h in range(2):
            for part in range(2):
                gath[tr, h, part * width : (part + 1) * width, :] = lead[
                    part, 0, :, h * half : (h + 1) * half
                ]
            ring_start(0, h)

    row = lax.broadcasted_iota(jnp.int32, (order, wide), 0)
    lane = lax.broadcasted_iota(jnp.int32, (order, wide), 1)
    chosen = jnp.logical_and(row == tr * width + lane, lane < width)
    unit = jnp.where(chosen, 1.0, 0.0).astype(jnp.bfloat16)
    for k in range(slabs):
        vec[k] = unit

    energy = energies[0]
    far = list(reversed(range(slabs, chains)))
    own = list(reversed(range(slabs)))

    def side_by_side(blocks):
        return blocks[0] if len(blocks) == 1 else jnp.concatenate(blocks, axis=1)

    def times(real_part, imag_part, value, span):
        by_real = mm(real_part, value)
        by_imag = mm(imag_part, value)
        blocks = []
        for base in range(0, value.shape[1], span):
            middle, end = base + span // 2, base + span
            blocks.append(by_real[:, base:middle] - by_imag[:, middle:end])
            blocks.append(by_real[:, middle:end] + by_imag[:, base:middle])
        return side_by_side(blocks)

    def times_seed(b, value):
        return times(sd[0, b], sd[1, b], value, wide)

    def back_stage(ks, b, fresh=False, pause=lambda: None):
        if fresh:
            for copy in inputs_of(b):
                copy.wait()
            couple_turned = jnp.transpose(cp[b])
            ct[b] = couple_turned
        u = times_seed(b, side_by_side([vec[k] for k in ks])).astype(jnp.bfloat16)
        for place, k in enumerate(ks):
            uvec[k, b] = u[:, place * wide : (place + 1) * wide]
        pause()
        before = mm(ct[b], u).astype(jnp.bfloat16)
        onsite = mm(hm[b], u)
        for place, k in enumerate(ks):
            block = slice(place * wide, (place + 1) * wide)
            vec[k] = before[:, block]
            u32 = u[:, block].astype(jnp.float32)
            turned = jnp.concatenate([-u32[:, pad:], u32[:, :pad]], axis=1)
            bias[k, b] = energy * u32 + broadening * turned - onsite[:, block]
        pause()

    def back_loop(ks):
        def body(i, carry):
            back_stage(ks, slabs - 1 - i)
            return carry

        lax.fori_loop(0, slabs, body, 0)

    def on_stage(ks, b):
        value = side_by_side([car[k] for k in ks])
        bent = side_by_side([bias[k, b] for k in ks])
        probe = (bent - mm(cp[b], value)).astype(jnp.bfloat16)
        twice = 2.0 * side_by_side([uvec[k, b] for k in ks]).astype(jnp.float32)
        green = (twice - times_seed(b, probe)).astype(jnp.bfloat16)
        for place, k in enumerate(ks):
            car[k] = green[:, place * wide : (place + 1) * wide]

    def on_loop(ks, count):
        def body(b, carry):
            on_stage(ks, b)
            return carry

        lax.fori_loop(0, count, body, 0)

    block_count = max(1, order // 256)
    block_width = order // block_count

    def left_start():
        def body(i, carry):
            cols = pl.ds(pl.multiple_of(i * block_width, 128), block_width)
            couple = cp[0, :, cols]
            for part in range(2):
                left[part, 0, :, cols] = mm(sd[part, 0], couple).astype(jnp.bfloat16)
            return carry

        lax.fori_loop(0, block_count, body, 0)

    def left_extend(b, i, pause=lambda place: None):
        cols = pl.ds(pl.multiple_of(i * block_width, 128), block_width)
        before = side_by_side([left[part, b - 1, :, cols] for part in range(2)])
        coupled = mm(cp[b], before).astype(jnp.bfloat16)
        pause(0)
        after = times(sd[0, b], sd[1, b], coupled, 2 * block_width).astype(jnp.bfloat16)
        left[0, b, :, cols] = after[:, :block_width]
        left[1, b, :, cols] = after[:, block_width:]
        pause(1)

    def affine_stage(ks, b):
        probe = side_by_side([bias[k, b] for k in ks])
        if b > 0:
            known = side_by_side([aff[k] for k in ks]).astype(jnp.bfloat16)
            probe = probe - mm(cp[b], known)
        twice = 2.0 * side_by_side([uvec[k, b] for k in ks]).astype(jnp.float32)
        green = twice - times_seed(b, probe.astype(jnp.bfloat16))
        for place, k in enumerate(ks):
            aff[k] = green[:, place * wide : (place + 1) * wide]

    def affine_loop(ks, b):
        def body(i, carry):
            affine_stage([ks[0] - i], b)
            return carry

        lax.fori_loop(0, len(ks), body, 0)

    def settle(k, b):
        car[k] = (aff[k] + times(left[0, b], left[1, b], car[k], wide)).astype(jnp.bfloat16)

    def emit(k):
        block = car[k]
        parts = [
            jnp.transpose(block[:, base : base + pad])[:width] for base in (0, pad)
        ]
        if k == slabs - 1:
            @pl.when(linked)
            def _():
                for h in range(2):
                    for part in range(2):
                        turned_out[h, part * width : (part + 1) * width, :] = parts[part][
                            :, h * half : (h + 1) * half
                        ]
                    send_block(h, seg + 1).start()

        for part in range(2):
            out[part, 0, k] = parts[part]

    def build(ks):
        def body(t, carry):
            rows = pl.ds(pl.multiple_of(t * width, 16), width)
            for k in ks:
                block = vec[k, rows, :]
                base = k * wide
                mix[t, 0:width, base : base + wide] = block
                mix[t, width : 2 * width, base : base + pad] = -block[:, pad:]
                mix[t, width : 2 * width, base + pad : base + wide] = block[:, :pad]
            return carry

        lax.fori_loop(0, n, body, 0)

    def gathered_times(ks):
        start, stop = min(ks) * wide, (max(ks) + 1) * wide
        for h in range(2):
            total = mm_left_turned(gath[0, h], mix[0, :, start:stop])
            for t in range(1, n):
                total = total + mm_left_turned(gath[t, h], mix[t, :, start:stop])
            total = total.astype(jnp.bfloat16)
            for k in ks:
                car[k, h * half : (h + 1) * half, :] = total[
                    :, k * wide - start : (k + 1) * wide - start
                ]

    @pl.when(high)
    def _():
        for k in own:
            for b in reversed(range(k + 1)):
                back_stage([k], b, fresh=k == slabs - 1)
            send_vec(k).start()

    @pl.when(seg == 1)
    def _():
        for k in own:
            send_car(k).wait_recv()
            on_loop([k], k + 1)
            emit(k)

    @pl.when(jnp.logical_and(high, seg > 1))
    def _():
        left_start()
        affine_loop(own, 0)
        for b in range(1, slabs):
            affine_loop(own[: slabs - b], b)

            def body(i, carry, b=b):
                left_extend(b, i)
                return carry

            lax.fori_loop(0, block_count, body, 0)
        for k in own:
            send_car(k).wait_recv()
            settle(k, k)
            emit(k)

    @pl.when(first)
    def _():
        waiting = list(range(ticks))

        def pause():
            if waiting:
                tick(waiting.pop(0))

        for b in own:
            back_stage(own[: slabs - b], b, fresh=True, pause=pause)
        send_vec(top - slabs).wait_recv()
        for b in own:
            back_stage([top], b, pause=pause)
        build([top])
        while waiting:
            pause()
        gathered_times([top])
        on_loop([top], slabs)
        send_car(top - slabs).start()
        for k in far[1:]:
            send_vec(k - slabs).wait_recv()
        back_loop(far[1:])
        build(far[1:] + own)
        gathered_times(far[1:] + own)
        on_loop(far[1:], slabs)
        for k in far[1:]:
            send_car(k - slabs).start()
        for b in range(slabs):
            on_stage(own[: slabs - b], b)
            emit(b)

    @pl.when(fed)
    def _():
        for b in own:
            back_stage(own[: slabs - b], b, fresh=True)
        for k in far:
            send_vec(k - slabs).wait_recv()
        back_loop(far)
        build(far + own)
        left_start()
        affine_loop(far + own, 0)
        for h in range(2):
            send_block(h, seg).wait_recv()
            ring_start(0, h)
        for h in range(2):
            acc[h] = mm_left_turned(gath[tr, h], mix[tr])

        def add(owner, h):
            acc[h] = acc[h] + mm_left_turned(gath[owner, h], mix[owner])

        def arrive(j):
            @pl.when(j < ticks)
            def _():
                tick(j)
                s, h = j // 2, j % 2
                when(goes_next(s, h))(lambda: add(tr_at(me - 1 - s), h))
                when(goes_prev(s, h))(lambda: add(tr_at(me + 1 + s), h))

        done = 0
        for b in range(1, slabs):
            def affine_body(i, carry, b=b, done=done):
                affine_stage([top - i], b)
                arrive(done + i)
                return carry

            lax.fori_loop(0, chains - b, affine_body, 0)
            done += chains - b

            def left_body(i, carry, b=b, done=done):
                left_extend(b, i, lambda place: arrive(done + 2 * i + place))
                return carry

            lax.fori_loop(0, block_count, left_body, 0)
            done += 2 * block_count

        def rest(j, carry):
            arrive(j)
            return carry

        if done < ticks:
            lax.fori_loop(done, ticks, rest, 0)
        for k in far + own:
            for h in range(2):
                car[k, h * half : (h + 1) * half, :] = acc[
                    h, :, k * wide : (k + 1) * wide
                ].astype(jnp.bfloat16)
            settle(k, min(k, slabs - 1))
            if k >= slabs:
                send_car(k - slabs).start()
            else:
                emit(k)

    @pl.when(high)
    def _():
        for k in range(slabs):
            send_vec(k).wait_send()

    @pl.when(linked)
    def _():
        for h in range(2):
            send_block(h, seg + 1).wait_send()

    @pl.when(low)
    def _():
        for k in range(slabs):
            send_car(k).wait_send()

        def sent(j, carry):
            s, h = j // 2, j % 2

            when(goes_next(s, h))(lambda: ring_next(s, h).wait_send())
            when(goes_prev(s, h))(lambda: ring_prev(s, h).wait_send())

            return carry

        lax.fori_loop(0, ticks, sent, 0)


def local(nseg, n, energies, hamiltonian, coupling, seed_inverse, lead_green):
    slabs, order, _ = hamiltonian.shape
    width = lead_green.shape[3]
    pad = -(-width // LANES) * LANES
    wide = 2 * pad
    chains = 2 * slabs
    steps = n // 2
    vmem = pl.BlockSpec(memory_space=pltpu.VMEM)
    anywhere = pl.BlockSpec(memory_space=pl.ANY)
    dma = pltpu.SemaphoreType.DMA
    bf16, f32 = jnp.bfloat16, jnp.float32
    turned = pl.pallas_call(
        functools.partial(kernel, nseg, n, width, pad),
        out_shape=jax.ShapeDtypeStruct((2, 1, slabs, width, order), bf16),
        in_specs=[pl.BlockSpec(memory_space=pltpu.SMEM)] + [anywhere] * 3 + [vmem],
        out_specs=vmem,
        scratch_shapes=[
            pltpu.VMEM((slabs, order, order), bf16),
            pltpu.VMEM((slabs, order, order), bf16),
            pltpu.VMEM((2, slabs, order, order), bf16),
            pltpu.VMEM((slabs, order, order), bf16),
            pltpu.VMEM((n, 2, 2 * width, order // 2), bf16),
            pltpu.VMEM((n, 2 * width, chains * wide), bf16),
            pltpu.VMEM((chains, order, wide), bf16),
            pltpu.VMEM((chains, slabs, order, wide), bf16),
            pltpu.VMEM((chains, slabs, order, wide), f32),
            pltpu.VMEM((2, order // 2, chains * wide), f32),
            pltpu.VMEM((chains, order, wide), bf16),
            pltpu.VMEM((2, 2 * width, order // 2), bf16),
            pltpu.VMEM((2, slabs, order, order), bf16),
            pltpu.VMEM((chains, order, wide), f32),
            dma((4, slabs)),
            dma((slabs,)), dma((slabs,)), dma((slabs,)), dma((slabs,)),
            dma((2,)), dma((2,)),
            dma((steps, 2)), dma((steps, 2)), dma((steps, 2)), dma((steps, 2)),
        ],
        compiler_params=pltpu.CompilerParams(
            collective_id=0, has_side_effects=True, vmem_limit_bytes=60 * 2**20
        ),
    )(energies, hamiltonian, coupling, seed_inverse, jnp.swapaxes(lead_green, 2, 3))
    return jnp.swapaxes(turned, 3, 4)


def solution(mesh):
    in_specs = (
        P(),
        P("seg", None, None),
        P("seg", None, None),
        P(None, None, "seg", None, None),
        P(None, None, None, "tr"),
    )
    out_specs = P(None, None, "seg", None, "tr")
    body = functools.partial(local, mesh.shape["seg"], mesh.shape["tr"])
    return jax.shard_map(body, mesh=mesh, in_specs=in_specs, out_specs=out_specs, check_vma=False)
```

```python
import functools

import jax
import jax.numpy as jnp
from jax import lax
from jax.experimental import pallas as pl
from jax.experimental.pallas import tpu as pltpu
from jax.sharding import PartitionSpec as P

broadening = 0.6
LANES = 128


def mm(left, right):
    return jnp.dot(left, right, preferred_element_type=jnp.float32)


def mm_left_turned(left, right):
    return lax.dot_general(
        left, right, (((0,), (0,)), ((), ())), preferred_element_type=jnp.float32
    )


def when(condition):
    if isinstance(condition, bool):
        return (lambda body: body()) if condition else (lambda body: None)
    return pl.when(condition)


def kernel(
    nseg, n, width, pad,
    energies, ham, cpl, seed, lead, out,
    hm, cp, sd, ct, gath, mix, vec, uvec, bias, acc, car, turned_out, left, aff,
    in_sem, vs_sem, vr_sem, cs_sem, cr_sem, gs_sem, gr_sem, fs_sem, fr_sem, bs_sem, br_sem,
):
    slabs = ham.shape[0]
    order = ham.shape[1]
    half = order // 2
    steps = n // 2
    ticks = 2 * steps
    wide = 2 * pad
    chains = 2 * slabs
    top = chains - 1
    seg = lax.axis_index("seg")
    tr = lax.axis_index("tr")
    role = seg % 2
    low = role == 0
    high = role == 1
    first = seg == 0
    partner = seg + 1 - 2 * role
    linked = jnp.logical_and(high, seg + 1 < nseg)
    fed = jnp.logical_and(low, seg > 0)

    def inputs_of(b):
        pairs = (
            (seed.at[0, 0, b], sd.at[0, b]),
            (seed.at[1, 0, b], sd.at[1, b]),
            (cpl.at[b], cp.at[b]),
            (ham.at[b], hm.at[b]),
        )
        return [
            pltpu.make_async_copy(src, dst, in_sem.at[place, b])
            for place, (src, dst) in enumerate(pairs)
        ]

    for b in reversed(range(slabs)):
        for copy in inputs_of(b):
            copy.start()

    def place_of(t):
        odd = t % 2
        return odd * (n - 1 - t // 2) + (1 - odd) * (t // 2)

    def tr_at(position):
        position = (position + 2 * n) % n
        past = position // steps
        return (1 - past) * (2 * position) + past * (2 * (n - 1 - position) + 1)

    me = place_of(tr)
    following, preceding = tr_at(me + 1), tr_at(me - 1)

    barrier = pltpu.get_barrier_semaphore()

    def greet(s, t):
        pl.semaphore_signal(
            barrier, inc=1, device_id=(s, t), device_id_type=pl.DeviceIdType.MESH
        )

    greet(partner, tr)

    @pl.when(low)
    def _():
        greet(seg, following)
        greet(seg, preceding)

    @pl.when(fed)
    def _():
        greet(seg - 1, tr)

    @pl.when(linked)
    def _():
        greet(seg + 1, tr)

    peers = 1 + 2 * (1 - role) + jnp.where(jnp.logical_or(fed, linked), 1, 0)
    pl.semaphore_wait(barrier, peers)

    def remote(src, dst, send, recv, s, t):
        return pltpu.make_async_remote_copy(
            src_ref=src, dst_ref=dst, send_sem=send, recv_sem=recv,
            device_id=(s, t), device_id_type=pl.DeviceIdType.MESH,
        )

    def ring_next(s, h):
        owner = tr_at(me - s)
        return remote(
            gath.at[owner, h], gath.at[owner, h], fs_sem.at[s, h], fr_sem.at[s, h], seg, following
        )

    def ring_prev(s, h):
        owner = tr_at(me + s)
        return remote(
            gath.at[owner, h], gath.at[owner, h], bs_sem.at[s, h], br_sem.at[s, h], seg, preceding
        )

    def goes_next(s, h):
        return (s < steps - 1) | (h == 0)

    def goes_prev(s, h):
        return (s < steps - 1) | (h == 1)

    def ring_start(s, h):
        when(goes_next(s, h))(lambda: ring_next(s, h).start())
        when(goes_prev(s, h))(lambda: ring_prev(s, h).start())

    def tick(j):
        s, h = j // 2, j % 2
        when(goes_next(s, h))(lambda: ring_next(s, h).wait_recv())
        when(goes_prev(s, h))(lambda: ring_prev(s, h).wait_recv())
        when(s + 1 < steps)(lambda: ring_start(s + 1, h))

    def send_vec(k):
        return remote(
            vec.at[k], vec.at[slabs + k], vs_sem.at[k], vr_sem.at[k], partner, tr
        )

    def send_car(k):
        return remote(
            car.at[slabs + k], car.at[k], cs_sem.at[k], cr_sem.at[k], partner, tr
        )

    def send_block(h, s):
        return remote(turned_out.at[h], gath.at[tr, h], gs_sem.at[h], gr_sem.at[h], s, tr)

    @pl.when(first)
    def _():
        for h in range(2):
            for part in range(2):
                gath[tr, h, part * width : (part + 1) * width, :] = lead[
                    part, 0, :, h * half : (h + 1) * half
                ]
            ring_start(0, h)

    row = lax.broadcasted_iota(jnp.int32, (order, wide), 0)
    lane = lax.broadcasted_iota(jnp.int32, (order, wide), 1)
    chosen = jnp.logical_and(row == tr * width + lane, lane < width)
    unit = jnp.where(chosen, 1.0, 0.0).astype(jnp.bfloat16)
    for k in range(slabs):
        vec[k] = unit

    energy = energies[0]
    far = list(reversed(range(slabs, chains)))
    own = list(reversed(range(slabs)))

    def side_by_side(blocks):
        return blocks[0] if len(blocks) == 1 else jnp.concatenate(blocks, axis=1)

    def times(real_part, imag_part, value, span):
        by_real = mm(real_part, value)
        by_imag = mm(imag_part, value)
        blocks = []
        for base in range(0, value.shape[1], span):
            middle, end = base + span // 2, base + span
            blocks.append(by_real[:, base:middle] - by_imag[:, middle:end])
            blocks.append(by_real[:, middle:end] + by_imag[:, base:middle])
        return side_by_side(blocks)

    def times_seed(b, value):
        return times(sd[0, b], sd[1, b], value, wide)

    def back_stage(ks, b, fresh=False, pause=lambda: None):
        if fresh:
            for copy in inputs_of(b):
                copy.wait()
            couple_turned = jnp.transpose(cp[b])
            ct[b] = couple_turned
        u = times_seed(b, side_by_side([vec[k] for k in ks])).astype(jnp.bfloat16)
        for place, k in enumerate(ks):
            uvec[k, b] = u[:, place * wide : (place + 1) * wide]
        pause()
        before = mm(ct[b], u).astype(jnp.bfloat16)
        onsite = mm(hm[b], u)
        for place, k in enumerate(ks):
            block = slice(place * wide, (place + 1) * wide)
            vec[k] = before[:, block]
            u32 = u[:, block].astype(jnp.float32)
            turned = jnp.concatenate([-u32[:, pad:], u32[:, :pad]], axis=1)
            bias[k, b] = energy * u32 + broadening * turned - onsite[:, block]
        pause()

    def back_loop(ks):
        def body(i, carry):
            back_stage(ks, slabs - 1 - i)
            return carry

        lax.fori_loop(0, slabs, body, 0)

    def on_stage(ks, b):
        value = side_by_side([car[k] for k in ks])
        bent = side_by_side([bias[k, b] for k in ks])
        probe = (bent - mm(cp[b], value)).astype(jnp.bfloat16)
        twice = 2.0 * side_by_side([uvec[k, b] for k in ks]).astype(jnp.float32)
        green = (twice - times_seed(b, probe)).astype(jnp.bfloat16)
        for place, k in enumerate(ks):
            car[k] = green[:, place * wide : (place + 1) * wide]

    def on_loop(ks, count):
        def body(b, carry):
            on_stage(ks, b)
            return carry

        lax.fori_loop(0, count, body, 0)

    block_count = max(1, order // 256)
    block_width = order // block_count

    def left_block(b, i):
        cols = pl.ds(pl.multiple_of(i * block_width, 128), block_width)
        couple = cp[b, :, cols]
        for part in range(2):
            left[part, b, :, cols] = mm(sd[part, b], couple).astype(jnp.bfloat16)

    def left_start():
        def body(i, carry):
            left_block(0, i)
            return carry

        lax.fori_loop(0, block_count, body, 0)

    def left_extend(b, i):
        cols = pl.ds(pl.multiple_of(i * block_width, 128), block_width)
        before = side_by_side([left[part, b - 1, :, cols] for part in range(2)])
        coupled = mm(cp[b], before).astype(jnp.bfloat16)
        after = times(sd[0, b], sd[1, b], coupled, 2 * block_width).astype(jnp.bfloat16)
        left[0, b, :, cols] = after[:, :block_width]
        left[1, b, :, cols] = after[:, block_width:]

    def affine_stage(ks, b):
        probe = side_by_side([bias[k, b] for k in ks])
        if b > 0:
            known = side_by_side([aff[k] for k in ks]).astype(jnp.bfloat16)
            probe = probe - mm(cp[b], known)
        twice = 2.0 * side_by_side([uvec[k, b] for k in ks]).astype(jnp.float32)
        green = twice - times_seed(b, probe.astype(jnp.bfloat16))
        for place, k in enumerate(ks):
            aff[k] = green[:, place * wide : (place + 1) * wide]

    def affine_loop(ks, b):
        def body(i, carry):
            affine_stage([ks[0] - i], b)
            return carry

        lax.fori_loop(0, len(ks), body, 0)

    def fold_stage(ks, b):
        probe = side_by_side([bias[k, b] for k in ks]).astype(jnp.bfloat16)
        twice = 2.0 * side_by_side([uvec[k, b] for k in ks]).astype(jnp.float32)
        folded = twice - times_seed(b, probe)
        for place, k in enumerate(ks):
            bias[k, b] = folded[:, place * wide : (place + 1) * wide]

    def fold_on(ks, b):
        value = side_by_side([car[k] for k in ks])
        folded = side_by_side([bias[k, b] for k in ks])
        green = (folded + times(left[0, b], left[1, b], value, wide)).astype(jnp.bfloat16)
        for place, k in enumerate(ks):
            car[k] = green[:, place * wide : (place + 1) * wide]

    def settle(k, b):
        car[k] = (aff[k] + times(left[0, b], left[1, b], car[k], wide)).astype(jnp.bfloat16)

    def emit(k):
        block = car[k]
        parts = [
            jnp.transpose(block[:, base : base + pad])[:width] for base in (0, pad)
        ]
        if k == slabs - 1:
            @pl.when(linked)
            def _():
                for h in range(2):
                    for part in range(2):
                        turned_out[h, part * width : (part + 1) * width, :] = parts[part][
                            :, h * half : (h + 1) * half
                        ]
                    send_block(h, seg + 1).start()

        for part in range(2):
            out[part, 0, k] = parts[part]

    def build(ks):
        def body(t, carry):
            rows = pl.ds(pl.multiple_of(t * width, 16), width)
            for k in ks:
                block = vec[k, rows, :]
                base = k * wide
                mix[t, 0:width, base : base + wide] = block
                mix[t, width : 2 * width, base : base + pad] = -block[:, pad:]
                mix[t, width : 2 * width, base + pad : base + wide] = block[:, :pad]
            return carry

        lax.fori_loop(0, n, body, 0)

    def gathered_times(ks):
        start, stop = min(ks) * wide, (max(ks) + 1) * wide
        for h in range(2):
            total = mm_left_turned(gath[0, h], mix[0, :, start:stop])
            for t in range(1, n):
                total = total + mm_left_turned(gath[t, h], mix[t, :, start:stop])
            total = total.astype(jnp.bfloat16)
            for k in ks:
                car[k, h * half : (h + 1) * half, :] = total[
                    :, k * wide - start : (k + 1) * wide - start
                ]

    @pl.when(high)
    def _():
        for k in own:
            for b in reversed(range(k + 1)):
                back_stage([k], b, fresh=k == slabs - 1)
            send_vec(k).start()

    @pl.when(seg == 1)
    def _():
        for k in own:
            send_car(k).wait_recv()
            on_loop([k], k + 1)
            emit(k)

    @pl.when(jnp.logical_and(high, seg > 1))
    def _():
        left_start()
        affine_loop(own, 0)
        for b in range(1, slabs):
            affine_loop(own[: slabs - b], b)

            def body(i, carry, b=b):
                left_extend(b, i)
                return carry

            lax.fori_loop(0, block_count, body, 0)
        for k in own:
            send_car(k).wait_recv()
            settle(k, k)
            emit(k)

    @pl.when(first)
    def _():
        waiting = list(range(ticks))

        def pause():
            if waiting:
                tick(waiting.pop(0))

        for b in own:
            back_stage(own[:1], b, fresh=True, pause=pause)
        send_vec(top - slabs).wait_recv()
        for b in own:
            back_stage([top], b, pause=pause)
        build([top])
        while waiting:
            pause()
        gathered_times([top])
        on_loop([top], slabs)
        send_car(top - slabs).start()
        for k in far[1:]:
            send_vec(k - slabs).wait_recv()
        for b in own:
            back_stage(far[1:] + [k for k in own[1:] if k >= b], b)
        build(far[1:] + own)
        gathered_times(far[1:] + own)
        on_loop(far[1:], slabs)
        for k in far[1:]:
            send_car(k - slabs).start()
        for b in range(slabs):
            on_stage(own[: slabs - b], b)
            emit(b)

    @pl.when(fed)
    def _():
        for b in own:
            back_stage(own[: slabs - b], b, fresh=True)
        for k in far:
            send_vec(k - slabs).wait_recv()
        back_loop(far)
        build(far + own)

        def fold_pair(i, carry):
            fold_stage([top - 2 * i, top - 2 * i - 1], 0)
            return carry

        lax.fori_loop(0, slabs, fold_pair, 0)
        for h in range(2):
            send_block(h, seg).wait_recv()
            ring_start(0, h)
        for h in range(2):
            acc[h] = mm_left_turned(gath[tr, h], mix[tr])

        def add(owner, h):
            acc[h] = acc[h] + mm_left_turned(gath[owner, h], mix[owner])

        def arrive(j):
            @pl.when(j < ticks)
            def _():
                tick(j)
                s, h = j // 2, j % 2
                when(goes_next(s, h))(lambda: add(tr_at(me - 1 - s), h))
                when(goes_prev(s, h))(lambda: add(tr_at(me + 1 + s), h))

        def left_body(i, carry):
            left_block(i // block_count, i % block_count)
            arrive(i)
            return carry

        done = slabs * block_count
        lax.fori_loop(0, done, left_body, 0)
        for b in range(1, slabs):
            def fold_body(i, carry, b=b, done=done):
                fold_stage([top - i], b)
                arrive(done + i)
                return carry

            lax.fori_loop(0, chains - b, fold_body, 0)
            done += chains - b

        def rest(j, carry):
            arrive(j)
            return carry

        if done < ticks:
            lax.fori_loop(done, ticks, rest, 0)
        for k in far + own:
            for h in range(2):
                car[k, h * half : (h + 1) * half, :] = acc[
                    h, :, k * wide : (k + 1) * wide
                ].astype(jnp.bfloat16)

        def fold_far(b, carry):
            fold_on(far, b)
            return carry

        lax.fori_loop(0, slabs, fold_far, 0)
        for k in far:
            send_car(k - slabs).start()
        for b in range(slabs):
            fold_on(own[: slabs - b], b)
            emit(b)

    @pl.when(high)
    def _():
        for k in range(slabs):
            send_vec(k).wait_send()

    @pl.when(linked)
    def _():
        for h in range(2):
            send_block(h, seg + 1).wait_send()

    @pl.when(low)
    def _():
        for k in range(slabs):
            send_car(k).wait_send()

        def sent(j, carry):
            s, h = j // 2, j % 2

            when(goes_next(s, h))(lambda: ring_next(s, h).wait_send())
            when(goes_prev(s, h))(lambda: ring_prev(s, h).wait_send())

            return carry

        lax.fori_loop(0, ticks, sent, 0)


def local(nseg, n, energies, hamiltonian, coupling, seed_inverse, lead_green):
    slabs, order, _ = hamiltonian.shape
    width = lead_green.shape[3]
    pad = -(-width // LANES) * LANES
    wide = 2 * pad
    chains = 2 * slabs
    steps = n // 2
    vmem = pl.BlockSpec(memory_space=pltpu.VMEM)
    anywhere = pl.BlockSpec(memory_space=pl.ANY)
    dma = pltpu.SemaphoreType.DMA
    bf16, f32 = jnp.bfloat16, jnp.float32
    turned = pl.pallas_call(
        functools.partial(kernel, nseg, n, width, pad),
        out_shape=jax.ShapeDtypeStruct((2, 1, slabs, width, order), bf16),
        in_specs=[pl.BlockSpec(memory_space=pltpu.SMEM)] + [anywhere] * 3 + [vmem],
        out_specs=vmem,
        scratch_shapes=[
            pltpu.VMEM((slabs, order, order), bf16),
            pltpu.VMEM((slabs, order, order), bf16),
            pltpu.VMEM((2, slabs, order, order), bf16),
            pltpu.VMEM((slabs, order, order), bf16),
            pltpu.VMEM((n, 2, 2 * width, order // 2), bf16),
            pltpu.VMEM((n, 2 * width, chains * wide), bf16),
            pltpu.VMEM((chains, order, wide), bf16),
            pltpu.VMEM((chains, slabs, order, wide), bf16),
            pltpu.VMEM((chains, slabs, order, wide), f32),
            pltpu.VMEM((2, order // 2, chains * wide), f32),
            pltpu.VMEM((chains, order, wide), bf16),
            pltpu.VMEM((2, 2 * width, order // 2), bf16),
            pltpu.VMEM((2, slabs, order, order), bf16),
            pltpu.VMEM((chains, order, wide), f32),
            dma((4, slabs)),
            dma((slabs,)), dma((slabs,)), dma((slabs,)), dma((slabs,)),
            dma((2,)), dma((2,)),
            dma((steps, 2)), dma((steps, 2)), dma((steps, 2)), dma((steps, 2)),
        ],
        compiler_params=pltpu.CompilerParams(
            collective_id=0, has_side_effects=True, vmem_limit_bytes=60 * 2**20
        ),
    )(energies, hamiltonian, coupling, seed_inverse, jnp.swapaxes(lead_green, 2, 3))
    return jnp.swapaxes(turned, 3, 4)


def solution(mesh):
    in_specs = (
        P(),
        P("seg", None, None),
        P("seg", None, None),
        P(None, None, "seg", None, None),
        P(None, None, None, "tr"),
    )
    out_specs = P(None, None, "seg", None, "tr")
    body = functools.partial(local, mesh.shape["seg"], mesh.shape["tr"])
    return jax.shard_map(body, mesh=mesh, in_specs=in_specs, out_specs=out_specs, check_vma=False)
```

```python
import functools

import jax
import jax.numpy as jnp
from jax import lax
from jax.experimental import pallas as pl
from jax.experimental.pallas import tpu as pltpu
from jax.sharding import PartitionSpec as P

broadening = 0.6
LANES = 128


def mm(left, right):
    return jnp.dot(left, right, preferred_element_type=jnp.float32)


def mm_left_turned(left, right):
    return lax.dot_general(
        left, right, (((0,), (0,)), ((), ())), preferred_element_type=jnp.float32
    )


def pick(index, values):
    total = jnp.int32(0)
    for place, value in enumerate(values):
        total = total + jnp.where(index == place, jnp.int32(value), jnp.int32(0))
    return total


def when(condition):
    if isinstance(condition, bool):
        return (lambda body: body()) if condition else (lambda body: None)
    return pl.when(condition)


def kernel(
    nseg, n, width, pad,
    energies, ham, cpl, seed, lead, out,
    hm, cp, sd, ct, gath, mix, vec, uvec, bias, acc, car, turned_out, left, aff, held,
    in_sem, vs_sem, vr_sem, cs_sem, cr_sem, gs_sem, gr_sem, fs_sem, fr_sem, bs_sem, br_sem,
):
    slabs = ham.shape[0]
    order = ham.shape[1]
    half = order // 2
    steps = n // 2
    ticks = 2 * steps
    wide = 2 * pad
    chains = 2 * slabs
    top = chains - 1
    seg = lax.axis_index("seg")
    tr = lax.axis_index("tr")
    role = seg % 2
    low = role == 0
    high = role == 1
    first = seg == 0
    partner = seg + 1 - 2 * role
    linked = jnp.logical_and(high, seg + 1 < nseg)
    fed = jnp.logical_and(low, seg > 0)

    def inputs_of(b):
        pairs = (
            (seed.at[0, 0, b], sd.at[0, b]),
            (seed.at[1, 0, b], sd.at[1, b]),
            (cpl.at[b], cp.at[b]),
            (ham.at[b], hm.at[b]),
        )
        return [
            pltpu.make_async_copy(src, dst, in_sem.at[place, b])
            for place, (src, dst) in enumerate(pairs)
        ]

    for b in reversed(range(slabs)):
        for copy in inputs_of(b):
            copy.start()

    def place_of(t):
        odd = t % 2
        return odd * (n - 1 - t // 2) + (1 - odd) * (t // 2)

    def tr_at(position):
        position = (position + 2 * n) % n
        past = position // steps
        return (1 - past) * (2 * position) + past * (2 * (n - 1 - position) + 1)

    me = place_of(tr)
    following, preceding = tr_at(me + 1), tr_at(me - 1)

    barrier = pltpu.get_barrier_semaphore()

    def greet(s, t):
        pl.semaphore_signal(
            barrier, inc=1, device_id=(s, t), device_id_type=pl.DeviceIdType.MESH
        )

    greet(partner, tr)

    @pl.when(low)
    def _():
        greet(seg, following)
        greet(seg, preceding)

    @pl.when(fed)
    def _():
        greet(seg - 1, tr)

    @pl.when(linked)
    def _():
        greet(seg + 1, tr)

    peers = 1 + 2 * (1 - role) + jnp.where(jnp.logical_or(fed, linked), 1, 0)
    pl.semaphore_wait(barrier, peers)

    def remote(src, dst, send, recv, s, t):
        return pltpu.make_async_remote_copy(
            src_ref=src, dst_ref=dst, send_sem=send, recv_sem=recv,
            device_id=(s, t), device_id_type=pl.DeviceIdType.MESH,
        )

    def ring_next(s, h):
        owner = tr_at(me - s)
        return remote(
            gath.at[owner, h], gath.at[owner, h], fs_sem.at[s, h], fr_sem.at[s, h], seg, following
        )

    def ring_prev(s, h):
        owner = tr_at(me + s)
        return remote(
            gath.at[owner, h], gath.at[owner, h], bs_sem.at[s, h], br_sem.at[s, h], seg, preceding
        )

    def goes_next(s, h):
        return (s < steps - 1) | (h == 0)

    def goes_prev(s, h):
        return (s < steps - 1) | (h == 1)

    def ring_start(s, h):
        when(goes_next(s, h))(lambda: ring_next(s, h).start())
        when(goes_prev(s, h))(lambda: ring_prev(s, h).start())

    def tick(j):
        s, h = j // 2, j % 2
        when(goes_next(s, h))(lambda: ring_next(s, h).wait_recv())
        when(goes_prev(s, h))(lambda: ring_prev(s, h).wait_recv())
        when(s + 1 < steps)(lambda: ring_start(s + 1, h))

    def send_vec(k):
        return remote(
            vec.at[k], vec.at[slabs + k], vs_sem.at[k], vr_sem.at[k], partner, tr
        )

    def send_car(k):
        return remote(
            car.at[slabs + k], car.at[k], cs_sem.at[k], cr_sem.at[k], partner, tr
        )

    def send_block(h, s):
        return remote(turned_out.at[h], gath.at[tr, h], gs_sem.at[h], gr_sem.at[h], s, tr)

    @pl.when(first)
    def _():
        for h in range(2):
            for part in range(2):
                gath[tr, h, part * width : (part + 1) * width, :] = lead[
                    part, 0, :, h * half : (h + 1) * half
                ]
            ring_start(0, h)

    row = lax.broadcasted_iota(jnp.int32, (order, wide), 0)
    lane = lax.broadcasted_iota(jnp.int32, (order, wide), 1)
    chosen = jnp.logical_and(row == tr * width + lane, lane < width)
    unit = jnp.where(chosen, 1.0, 0.0).astype(jnp.bfloat16)
    for k in range(slabs):
        vec[k] = unit

    energy = energies[0]
    far = list(reversed(range(slabs, chains)))
    own = list(reversed(range(slabs)))

    def side_by_side(blocks):
        return blocks[0] if len(blocks) == 1 else jnp.concatenate(blocks, axis=1)

    def times(real_part, imag_part, value, span):
        by_real = mm(real_part, value)
        by_imag = mm(imag_part, value)
        blocks = []
        for base in range(0, value.shape[1], span):
            middle, end = base + span // 2, base + span
            blocks.append(by_real[:, base:middle] - by_imag[:, middle:end])
            blocks.append(by_real[:, middle:end] + by_imag[:, base:middle])
        return side_by_side(blocks)

    def by_halves(body):
        def run(h, carry):
            body(pl.ds(pl.multiple_of(h * half, 16), half))
            return carry

        lax.fori_loop(0, 2, run, 0)

    def times_seed(b, rows, value):
        return times(sd[0, b, rows, :], sd[1, b, rows, :], value, wide)

    def twice(k, b, rows):
        return 2.0 * uvec[k, b, rows, :].astype(jnp.float32)

    def back_stage(k, b, pause=lambda place: None):
        def seeded(rows):
            uvec[k, b, rows, :] = times_seed(b, rows, vec[k]).astype(jnp.bfloat16)

        by_halves(seeded)
        pause(0)

        def coupled(rows):
            u = uvec[k, b]
            vec[k, rows, :] = mm(ct[b, rows, :], u).astype(jnp.bfloat16)
            u32 = uvec[k, b, rows, :].astype(jnp.float32)
            turned = jnp.concatenate([-u32[:, pad:], u32[:, :pad]], axis=1)
            bias[k, b, rows, :] = energy * u32 + broadening * turned - mm(hm[b, rows, :], u)

        by_halves(coupled)
        pause(1)

    def on_stage(k, b):
        def probed(rows):
            probe = bias[k, b, rows, :] - mm(cp[b, rows, :], car[k])
            held[rows, :] = probe.astype(jnp.bfloat16)

        by_halves(probed)

        def finished(rows):
            green = twice(k, b, rows) - times_seed(b, rows, held[...])
            car[k, rows, :] = green.astype(jnp.bfloat16)

        by_halves(finished)

    block_count = max(1, order // 256)
    block_width = order // block_count

    def left_block(b, i):
        cols = pl.ds(pl.multiple_of(i * block_width, 128), block_width)
        couple = cp[b, :, cols]
        for part in range(2):
            left[part, b, :, cols] = mm(sd[part, b], couple).astype(jnp.bfloat16)

    def left_start():
        def body(i, carry):
            left_block(0, i)
            return carry

        lax.fori_loop(0, block_count, body, 0)

    def left_extend(b, i):
        cols = pl.ds(pl.multiple_of(i * block_width, 128), block_width)
        before = side_by_side([left[part, b - 1, :, cols] for part in range(2)])
        coupled = mm(cp[b], before).astype(jnp.bfloat16)

        def extended(rows):
            after = times(sd[0, b, rows, :], sd[1, b, rows, :], coupled, 2 * block_width)
            after = after.astype(jnp.bfloat16)
            left[0, b, rows, cols] = after[:, :block_width]
            left[1, b, rows, cols] = after[:, block_width:]

        by_halves(extended)

    def affine_stage(k, b):
        if b == 0:
            held[...] = bias[k, 0].astype(jnp.bfloat16)
        else:
            known = aff[k].astype(jnp.bfloat16)
            held[...] = (bias[k, b] - mm(cp[b], known)).astype(jnp.bfloat16)

        def finished(rows):
            aff[k, rows, :] = twice(k, b, rows) - times_seed(b, rows, held[...])

        by_halves(finished)

    def affine_loop(ks, b):
        def body(i, carry):
            affine_stage(ks[0] - i, b)
            return carry

        lax.fori_loop(0, len(ks), body, 0)

    def fold_stage(k, b):
        held[...] = bias[k, b].astype(jnp.bfloat16)

        def folded(rows):
            bias[k, b, rows, :] = twice(k, b, rows) - times_seed(b, rows, held[...])

        by_halves(folded)

    def fold_on(k, b):
        held[...] = car[k]

        def finished(rows):
            value = times(left[0, b, rows, :], left[1, b, rows, :], held[...], wide)
            car[k, rows, :] = (bias[k, b, rows, :] + value).astype(jnp.bfloat16)

        by_halves(finished)

    def settle(k, b):
        held[...] = car[k]

        def finished(rows):
            value = times(left[0, b, rows, :], left[1, b, rows, :], held[...], wide)
            car[k, rows, :] = (aff[k, rows, :] + value).astype(jnp.bfloat16)

        by_halves(finished)

    def emit(k):
        block = car[k]
        parts = [
            jnp.transpose(block[:, base : base + pad])[:width] for base in (0, pad)
        ]
        if k == slabs - 1:
            @pl.when(linked)
            def _():
                for h in range(2):
                    for part in range(2):
                        turned_out[h, part * width : (part + 1) * width, :] = parts[part][
                            :, h * half : (h + 1) * half
                        ]
                    send_block(h, seg + 1).start()

        for part in range(2):
            out[part, 0, k] = parts[part]

    def build(ks):
        def body(t, carry):
            rows = pl.ds(pl.multiple_of(t * width, 16), width)
            for k in ks:
                block = vec[k, rows, :]
                base = k * wide
                mix[t, 0:width, base : base + wide] = block
                mix[t, width : 2 * width, base : base + pad] = -block[:, pad:]
                mix[t, width : 2 * width, base + pad : base + wide] = block[:, :pad]
            return carry

        lax.fori_loop(0, n, body, 0)

    def gathered_times(ks):
        start, stop = min(ks) * wide, (max(ks) + 1) * wide

        def body(h, carry):
            total = mm_left_turned(gath[0, h], mix[0, :, start:stop])
            for t in range(1, n):
                total = total + mm_left_turned(gath[t, h], mix[t, :, start:stop])
            total = total.astype(jnp.bfloat16)
            rows = pl.ds(pl.multiple_of(h * half, 16), half)
            for k in ks:
                car[k, rows, :] = total[:, k * wide - start : (k + 1) * wide - start]
            return carry

        lax.fori_loop(0, 2, body, 0)

    def down(k):
        return [(k, b) for b in reversed(range(min(k + 1, slabs)))]

    main = down(slabs - 1) + down(top)
    rest_own = [item for k in own[1:] for item in down(k)]
    rest_far = [item for k in far[1:] for item in down(k)]
    plan = main + rest_own + rest_far
    last_tick = min(ticks, 2 * len(main))

    def plan_pass(i):
        k = pick(i, [item[0] for item in plan])
        b = pick(i, [item[1] for item in plan])

        @pl.when(i < slabs)
        def _():
            for copy in inputs_of(b):
                copy.wait()
            ct[b] = jnp.transpose(cp[b])

        for index, (chain, slab) in enumerate(plan):
            if chain >= slabs and slab == slabs - 1:
                @pl.when(i == index)
                def _(chain=chain):
                    send_vec(chain - slabs).wait_recv()

        def pause(place):
            j = 2 * i + place

            @pl.when(jnp.logical_and(first, j < last_tick))
            def _():
                tick(j)

        back_stage(k, b, pause)
        for index, (chain, slab) in enumerate(plan):
            if chain < slabs and slab == 0:
                @pl.when(jnp.logical_and(high, i == index))
                def _(chain=chain):
                    send_vec(chain).start()

    def opening(i, carry):
        plan_pass(jnp.where(jnp.logical_and(high, i >= slabs), i + slabs, i))
        return carry

    own_count = slabs + len(rest_own)
    opening_count = jnp.where(high, own_count, jnp.where(first, len(main), len(plan)))
    lax.fori_loop(0, opening_count, opening, 0)

    onward = [(k, b) for k in far[1:] for b in range(slabs)]
    far_rest = len(onward)
    onward = onward + [(k, b) for k in own for b in range(k + 1)]

    def onward_pass(i, carry):
        k = pick(i, [item[0] for item in onward])
        b = pick(i, [item[1] for item in onward])
        for index, (chain, slab) in enumerate(onward):
            if chain < slabs and slab == 0:
                @pl.when(jnp.logical_and(high, i == index))
                def _(chain=chain):
                    send_car(chain).wait_recv()

        on_stage(k, b)
        for index, (chain, slab) in enumerate(onward):
            if chain >= slabs and slab == slabs - 1:
                @pl.when(i == index)
                def _(chain=chain):
                    send_car(chain - slabs).start()

            if chain == slab:
                @pl.when(i == index)
                def _(chain=chain):
                    emit(chain)

        return carry

    @pl.when(jnp.logical_and(high, seg > 1))
    def _():
        left_start()
        affine_loop(own, 0)
        for b in range(1, slabs):
            affine_loop(own[: slabs - b], b)

            def body(i, carry, b=b):
                left_extend(b, i)
                return carry

            lax.fori_loop(0, block_count, body, 0)
        for k in own:
            send_car(k).wait_recv()
            settle(k, k)
            emit(k)

    @pl.when(first)
    def _():
        build([top])

        def flush(j, carry):
            tick(j)
            return carry

        if last_tick < ticks:
            lax.fori_loop(last_tick, ticks, flush, 0)
        gathered_times([top])

        def main_on(b, carry):
            on_stage(top, b)
            return carry

        lax.fori_loop(0, slabs, main_on, 0)
        send_car(top - slabs).start()

        def later(i, carry):
            plan_pass(i)
            return carry

        lax.fori_loop(len(main), len(plan), later, 0)
        build(far[1:] + own)
        gathered_times(far[1:] + own)

    @pl.when(seg < 2)
    def _():
        lax.fori_loop(role * far_rest, len(onward), onward_pass, 0)

    @pl.when(fed)
    def _():
        build(far + own)

        def fold_one(i, carry):
            fold_stage(top - i, 0)
            return carry

        lax.fori_loop(0, chains, fold_one, 0)
        for h in range(2):
            send_block(h, seg).wait_recv()
            ring_start(0, h)
        for h in range(2):
            acc[h] = mm_left_turned(gath[tr, h], mix[tr])

        def add(owner, h):
            acc[h] = acc[h] + mm_left_turned(gath[owner, h], mix[owner])

        def arrive(j):
            @pl.when(j < ticks)
            def _():
                tick(j)
                s, h = j // 2, j % 2
                when(goes_next(s, h))(lambda: add(tr_at(me - 1 - s), h))
                when(goes_prev(s, h))(lambda: add(tr_at(me + 1 + s), h))

        def left_body(i, carry):
            left_block(i // block_count, i % block_count)
            arrive(i)
            return carry

        done = slabs * block_count
        lax.fori_loop(0, done, left_body, 0)
        for b in range(1, slabs):
            def fold_body(i, carry, b=b, done=done):
                fold_stage(top - i, b)
                arrive(done + i)
                return carry

            lax.fori_loop(0, chains - b, fold_body, 0)
            done += chains - b

        def rest(j, carry):
            arrive(j)
            return carry

        if done < ticks:
            lax.fori_loop(done, ticks, rest, 0)
        for k in far + own:
            for h in range(2):
                car[k, h * half : (h + 1) * half, :] = acc[
                    h, :, k * wide : (k + 1) * wide
                ].astype(jnp.bfloat16)

        closing = [(k, b) for k in far for b in range(slabs)]
        closing = closing + [(k, b) for k in own for b in range(k + 1)]

        def closing_pass(i, carry):
            k = pick(i, [item[0] for item in closing])
            b = pick(i, [item[1] for item in closing])
            fold_on(k, b)
            for index, (chain, slab) in enumerate(closing):
                if chain >= slabs and slab == slabs - 1:
                    @pl.when(i == index)
                    def _(chain=chain):
                        send_car(chain - slabs).start()

                if chain == slab:
                    @pl.when(i == index)
                    def _(chain=chain):
                        emit(chain)

            return carry

        lax.fori_loop(0, len(closing), closing_pass, 0)

    @pl.when(high)
    def _():
        for k in range(slabs):
            send_vec(k).wait_send()

    @pl.when(linked)
    def _():
        for h in range(2):
            send_block(h, seg + 1).wait_send()

    @pl.when(low)
    def _():
        for k in range(slabs):
            send_car(k).wait_send()

        def sent(j, carry):
            s, h = j // 2, j % 2

            when(goes_next(s, h))(lambda: ring_next(s, h).wait_send())
            when(goes_prev(s, h))(lambda: ring_prev(s, h).wait_send())

            return carry

        lax.fori_loop(0, ticks, sent, 0)


def local(nseg, n, energies, hamiltonian, coupling, seed_inverse, lead_green):
    slabs, order, _ = hamiltonian.shape
    width = lead_green.shape[3]
    pad = -(-width // LANES) * LANES
    wide = 2 * pad
    chains = 2 * slabs
    steps = n // 2
    vmem = pl.BlockSpec(memory_space=pltpu.VMEM)
    anywhere = pl.BlockSpec(memory_space=pl.ANY)
    dma = pltpu.SemaphoreType.DMA
    bf16, f32 = jnp.bfloat16, jnp.float32
    turned = pl.pallas_call(
        functools.partial(kernel, nseg, n, width, pad),
        out_shape=jax.ShapeDtypeStruct((2, 1, slabs, width, order), bf16),
        in_specs=[pl.BlockSpec(memory_space=pltpu.SMEM)] + [anywhere] * 3 + [vmem],
        out_specs=vmem,
        scratch_shapes=[
            pltpu.VMEM((slabs, order, order), bf16),
            pltpu.VMEM((slabs, order, order), bf16),
            pltpu.VMEM((2, slabs, order, order), bf16),
            pltpu.VMEM((slabs, order, order), bf16),
            pltpu.VMEM((n, 2, 2 * width, order // 2), bf16),
            pltpu.VMEM((n, 2 * width, chains * wide), bf16),
            pltpu.VMEM((chains, order, wide), bf16),
            pltpu.VMEM((chains, slabs, order, wide), bf16),
            pltpu.VMEM((chains, slabs, order, wide), f32),
            pltpu.VMEM((2, order // 2, chains * wide), f32),
            pltpu.VMEM((chains, order, wide), bf16),
            pltpu.VMEM((2, 2 * width, order // 2), bf16),
            pltpu.VMEM((2, slabs, order, order), bf16),
            pltpu.VMEM((chains, order, wide), f32),
            pltpu.VMEM((order, wide), bf16),
            dma((4, slabs)),
            dma((slabs,)), dma((slabs,)), dma((slabs,)), dma((slabs,)),
            dma((2,)), dma((2,)),
            dma((steps, 2)), dma((steps, 2)), dma((steps, 2)), dma((steps, 2)),
        ],
        compiler_params=pltpu.CompilerParams(
            collective_id=0, has_side_effects=True, vmem_limit_bytes=60 * 2**20
        ),
    )(energies, hamiltonian, coupling, seed_inverse, jnp.swapaxes(lead_green, 2, 3))
    return jnp.swapaxes(turned, 3, 4)


def solution(mesh):
    in_specs = (
        P(),
        P("seg", None, None),
        P("seg", None, None),
        P(None, None, "seg", None, None),
        P(None, None, None, "tr"),
    )
    out_specs = P(None, None, "seg", None, "tr")
    body = functools.partial(local, mesh.shape["seg"], mesh.shape["tr"])
    return jax.shard_map(body, mesh=mesh, in_specs=in_specs, out_specs=out_specs, check_vma=False)
```

```python
import functools

import jax
import jax.numpy as jnp
from jax import lax
from jax.experimental import pallas as pl
from jax.experimental.pallas import tpu as pltpu
from jax.sharding import PartitionSpec as P

broadening = 0.6
LANES = 128


def mm(left, right):
    return jnp.dot(left, right, preferred_element_type=jnp.float32)


def mm_left_turned(left, right):
    return lax.dot_general(
        left, right, (((0,), (0,)), ((), ())), preferred_element_type=jnp.float32
    )


def when(condition):
    if isinstance(condition, bool):
        return (lambda body: body()) if condition else (lambda body: None)
    return pl.when(condition)


def kernel(
    nseg, n, width, pad,
    energies, ham, cpl, seed, lead, out,
    hm, cp, sd, ct, gath, mix, vec, uvec, bias, acc, car, turned_out, left, aff,
    in_sem, vs_sem, vr_sem, cs_sem, cr_sem, gs_sem, gr_sem, fs_sem, fr_sem, bs_sem, br_sem,
):
    slabs = ham.shape[0]
    order = ham.shape[1]
    half = order // 2
    steps = n // 2
    ticks = 2 * steps
    wide = 2 * pad
    chains = 2 * slabs
    top = chains - 1
    seg = lax.axis_index("seg")
    tr = lax.axis_index("tr")
    role = seg % 2
    low = role == 0
    high = role == 1
    first = seg == 0
    partner = seg + 1 - 2 * role
    linked = jnp.logical_and(high, seg + 1 < nseg)
    fed = jnp.logical_and(low, seg > 0)

    def inputs_of(b):
        pairs = (
            (seed.at[0, 0, b], sd.at[0, b]),
            (seed.at[1, 0, b], sd.at[1, b]),
            (cpl.at[b], cp.at[b]),
            (ham.at[b], hm.at[b]),
        )
        return [
            pltpu.make_async_copy(src, dst, in_sem.at[place, b])
            for place, (src, dst) in enumerate(pairs)
        ]

    for b in reversed(range(slabs)):
        for copy in inputs_of(b):
            copy.start()

    def place_of(t):
        odd = t % 2
        return odd * (n - 1 - t // 2) + (1 - odd) * (t // 2)

    def tr_at(position):
        position = (position + 2 * n) % n
        past = position // steps
        return (1 - past) * (2 * position) + past * (2 * (n - 1 - position) + 1)

    me = place_of(tr)
    following, preceding = tr_at(me + 1), tr_at(me - 1)

    barrier = pltpu.get_barrier_semaphore()

    def greet(s, t):
        pl.semaphore_signal(
            barrier, inc=1, device_id=(s, t), device_id_type=pl.DeviceIdType.MESH
        )

    greet(partner, tr)

    @pl.when(low)
    def _():
        greet(seg, following)
        greet(seg, preceding)

    @pl.when(fed)
    def _():
        greet(seg - 1, tr)

    @pl.when(linked)
    def _():
        greet(seg + 1, tr)

    peers = 1 + 2 * (1 - role) + jnp.where(jnp.logical_or(fed, linked), 1, 0)
    pl.semaphore_wait(barrier, peers)

    def remote(src, dst, send, recv, s, t):
        return pltpu.make_async_remote_copy(
            src_ref=src, dst_ref=dst, send_sem=send, recv_sem=recv,
            device_id=(s, t), device_id_type=pl.DeviceIdType.MESH,
        )

    def ring_next(s, h):
        owner = tr_at(me - s)
        return remote(
            gath.at[owner, h], gath.at[owner, h], fs_sem.at[s, h], fr_sem.at[s, h], seg, following
        )

    def ring_prev(s, h):
        owner = tr_at(me + s)
        return remote(
            gath.at[owner, h], gath.at[owner, h], bs_sem.at[s, h], br_sem.at[s, h], seg, preceding
        )

    def goes_next(s, h):
        return (s < steps - 1) | (h == 0)

    def goes_prev(s, h):
        return (s < steps - 1) | (h == 1)

    def ring_start(s, h):
        when(goes_next(s, h))(lambda: ring_next(s, h).start())
        when(goes_prev(s, h))(lambda: ring_prev(s, h).start())

    def tick(j):
        s, h = j // 2, j % 2
        when(goes_next(s, h))(lambda: ring_next(s, h).wait_recv())
        when(goes_prev(s, h))(lambda: ring_prev(s, h).wait_recv())
        when(s + 1 < steps)(lambda: ring_start(s + 1, h))

    def send_vec(k):
        return remote(
            vec.at[k], vec.at[slabs + k], vs_sem.at[k], vr_sem.at[k], partner, tr
        )

    def send_car(k):
        return remote(
            car.at[slabs + k], car.at[k], cs_sem.at[k], cr_sem.at[k], partner, tr
        )

    def send_block(h, s):
        return remote(turned_out.at[h], gath.at[tr, h], gs_sem.at[h], gr_sem.at[h], s, tr)

    @pl.when(first)
    def _():
        for h in range(2):
            for part in range(2):
                gath[tr, h, part * width : (part + 1) * width, :] = lead[
                    part, 0, :, h * half : (h + 1) * half
                ]
            ring_start(0, h)

    row = lax.broadcasted_iota(jnp.int32, (order, wide), 0)
    lane = lax.broadcasted_iota(jnp.int32, (order, wide), 1)
    chosen = jnp.logical_and(row == tr * width + lane, lane < width)
    unit = jnp.where(chosen, 1.0, 0.0).astype(jnp.bfloat16)
    for k in range(slabs):
        vec[k] = unit

    energy = energies[0]
    far = list(reversed(range(slabs, chains)))
    own = list(reversed(range(slabs)))

    def side_by_side(blocks):
        return blocks[0] if len(blocks) == 1 else jnp.concatenate(blocks, axis=1)

    def times(real_part, imag_part, value, span):
        by_real = mm(real_part, value)
        by_imag = mm(imag_part, value)
        blocks = []
        for base in range(0, value.shape[1], span):
            middle, end = base + span // 2, base + span
            blocks.append(by_real[:, base:middle] - by_imag[:, middle:end])
            blocks.append(by_real[:, middle:end] + by_imag[:, base:middle])
        return side_by_side(blocks)

    def times_seed(b, value):
        return times(sd[0, b], sd[1, b], value, wide)

    def back_stage(ks, b, fresh=False, pause=lambda: None):
        if fresh:
            for copy in inputs_of(b):
                copy.wait()
            couple_turned = jnp.transpose(cp[b])
            ct[b] = couple_turned
        u = times_seed(b, side_by_side([vec[k] for k in ks])).astype(jnp.bfloat16)
        for place, k in enumerate(ks):
            uvec[k, b] = u[:, place * wide : (place + 1) * wide]
        pause()
        before = mm(ct[b], u).astype(jnp.bfloat16)
        onsite = mm(hm[b], u)
        for place, k in enumerate(ks):
            block = slice(place * wide, (place + 1) * wide)
            vec[k] = before[:, block]
            u32 = u[:, block].astype(jnp.float32)
            turned = jnp.concatenate([-u32[:, pad:], u32[:, :pad]], axis=1)
            bias[k, b] = energy * u32 + broadening * turned - onsite[:, block]
        pause()

    def back_loop(ks):
        def body(i, carry):
            back_stage(ks, slabs - 1 - i)
            return carry

        lax.fori_loop(0, slabs, body, 0)

    def on_stage(ks, b):
        value = side_by_side([car[k] for k in ks])
        bent = side_by_side([bias[k, b] for k in ks])
        probe = (bent - mm(cp[b], value)).astype(jnp.bfloat16)
        twice = 2.0 * side_by_side([uvec[k, b] for k in ks]).astype(jnp.float32)
        green = (twice - times_seed(b, probe)).astype(jnp.bfloat16)
        for place, k in enumerate(ks):
            car[k] = green[:, place * wide : (place + 1) * wide]

    def on_loop(ks, count):
        def body(b, carry):
            on_stage(ks, b)
            return carry

        lax.fori_loop(0, count, body, 0)

    block_count = max(1, order // 256)
    block_width = order // block_count

    def left_start():
        def body(i, carry):
            cols = pl.ds(pl.multiple_of(i * block_width, 128), block_width)
            couple = cp[0, :, cols]
            for part in range(2):
                left[part, 0, :, cols] = mm(sd[part, 0], couple).astype(jnp.bfloat16)
            return carry

        lax.fori_loop(0, block_count, body, 0)

    def left_extend(b, i, pause=lambda place: None):
        cols = pl.ds(pl.multiple_of(i * block_width, 128), block_width)
        before = side_by_side([left[part, b - 1, :, cols] for part in range(2)])
        coupled = mm(cp[b], before).astype(jnp.bfloat16)
        pause(0)
        after = times(sd[0, b], sd[1, b], coupled, 2 * block_width).astype(jnp.bfloat16)
        left[0, b, :, cols] = after[:, :block_width]
        left[1, b, :, cols] = after[:, block_width:]
        pause(1)

    def affine_stage(ks, b):
        probe = side_by_side([bias[k, b] for k in ks])
        if b > 0:
            known = side_by_side([aff[k] for k in ks]).astype(jnp.bfloat16)
            probe = probe - mm(cp[b], known)
        twice = 2.0 * side_by_side([uvec[k, b] for k in ks]).astype(jnp.float32)
        green = twice - times_seed(b, probe.astype(jnp.bfloat16))
        for place, k in enumerate(ks):
            aff[k] = green[:, place * wide : (place + 1) * wide]

    def affine_loop(ks, b):
        def body(i, carry):
            affine_stage([ks[0] - i], b)
            return carry

        lax.fori_loop(0, len(ks), body, 0)

    def settle(k, b):
        car[k] = (aff[k] + times(left[0, b], left[1, b], car[k], wide)).astype(jnp.bfloat16)

    def emit(k):
        block = car[k]
        parts = [
            jnp.transpose(block[:, base : base + pad])[:width] for base in (0, pad)
        ]
        if k == slabs - 1:
            @pl.when(linked)
            def _():
                for h in range(2):
                    for part in range(2):
                        turned_out[h, part * width : (part + 1) * width, :] = parts[part][
                            :, h * half : (h + 1) * half
                        ]
                    send_block(h, seg + 1).start()

        for part in range(2):
            out[part, 0, k] = parts[part]

    def build(ks):
        def body(t, carry):
            rows = pl.ds(pl.multiple_of(t * width, 16), width)
            for k in ks:
                block = vec[k, rows, :]
                base = k * wide
                mix[t, 0:width, base : base + wide] = block
                mix[t, width : 2 * width, base : base + pad] = -block[:, pad:]
                mix[t, width : 2 * width, base + pad : base + wide] = block[:, :pad]
            return carry

        lax.fori_loop(0, n, body, 0)

    def gathered_times(ks):
        start, stop = min(ks) * wide, (max(ks) + 1) * wide
        for h in range(2):
            total = mm_left_turned(gath[0, h], mix[0, :, start:stop])
            for t in range(1, n):
                total = total + mm_left_turned(gath[t, h], mix[t, :, start:stop])
            total = total.astype(jnp.bfloat16)
            for k in ks:
                car[k, h * half : (h + 1) * half, :] = total[
                    :, k * wide - start : (k + 1) * wide - start
                ]

    @pl.when(high)
    def _():
        for k in own:
            for b in reversed(range(k + 1)):
                back_stage([k], b, fresh=k == slabs - 1)
            send_vec(k).start()

    @pl.when(seg == 1)
    def _():
        for k in own:
            send_car(k).wait_recv()
            on_loop([k], k + 1)
            emit(k)

    @pl.when(jnp.logical_and(high, seg > 1))
    def _():
        left_start()
        affine_loop(own, 0)
        for b in range(1, slabs):
            affine_loop(own[: slabs - b], b)

            def body(i, carry, b=b):
                left_extend(b, i)
                return carry

            lax.fori_loop(0, block_count, body, 0)
        for k in own:
            send_car(k).wait_recv()
            settle(k, k)
            emit(k)

    @pl.when(first)
    def _():
        waiting = list(range(ticks))

        def pause():
            if waiting:
                tick(waiting.pop(0))

        for b in own:
            back_stage(own[:1], b, fresh=True, pause=pause)
        send_vec(top - slabs).wait_recv()
        for b in own:
            back_stage([top], b, pause=pause)
        build([top])
        while waiting:
            pause()
        gathered_times([top])
        on_loop([top], slabs)
        send_car(top - slabs).start()
        for k in far[1:]:
            send_vec(k - slabs).wait_recv()
        for b in own:
            back_stage(far[1:] + [k for k in own[1:] if k >= b], b)
        build(far[1:] + own)
        gathered_times(far[1:] + own)
        on_loop(far[1:], slabs)
        for k in far[1:]:
            send_car(k - slabs).start()
        for b in range(slabs):
            on_stage(own[: slabs - b], b)
            emit(b)

    @pl.when(fed)
    def _():
        for b in own:
            back_stage(own[: slabs - b], b, fresh=True)
        for k in far:
            send_vec(k - slabs).wait_recv()
        back_loop(far)
        build(far + own)
        left_start()

        def affine_pair(i, carry):
            affine_stage([top - 2 * i, top - 2 * i - 1], 0)
            return carry

        lax.fori_loop(0, slabs, affine_pair, 0)
        for h in range(2):
            send_block(h, seg).wait_recv()
            ring_start(0, h)
        for h in range(2):
            acc[h] = mm_left_turned(gath[tr, h], mix[tr])

        def add(owners, h):
            total = mm_left_turned(gath[owners[0], h], mix[owners[0]])
            for owner in owners[1:]:
                total = total + mm_left_turned(gath[owner, h], mix[owner])
            acc[h] = acc[h] + total

        def arrive(j):
            @pl.when(j < ticks)
            def _():
                tick(j)
                s, h = j // 2, j % 2
                when(s < steps - 1)(lambda: add((tr_at(me - 1 - s), tr_at(me + 1 + s)), h))
                when(s == steps - 1)(lambda: add((tr_at(me + steps),), h))

        done = 0
        for b in range(1, slabs):
            def affine_body(i, carry, b=b, done=done):
                affine_stage([top - i], b)
                arrive(done + i)
                return carry

            lax.fori_loop(0, chains - b, affine_body, 0)
            done += chains - b

            def left_body(i, carry, b=b, done=done):
                left_extend(b, i, lambda place: arrive(done + 2 * i + place))
                return carry

            lax.fori_loop(0, block_count, left_body, 0)
            done += 2 * block_count

        def rest(j, carry):
            arrive(j)
            return carry

        if done < ticks:
            lax.fori_loop(done, ticks, rest, 0)
        for k in far + own:
            for h in range(2):
                car[k, h * half : (h + 1) * half, :] = acc[
                    h, :, k * wide : (k + 1) * wide
                ].astype(jnp.bfloat16)
            settle(k, min(k, slabs - 1))
            if k >= slabs:
                send_car(k - slabs).start()
            else:
                emit(k)

    @pl.when(high)
    def _():
        for k in range(slabs):
            send_vec(k).wait_send()

    @pl.when(linked)
    def _():
        for h in range(2):
            send_block(h, seg + 1).wait_send()

    @pl.when(low)
    def _():
        for k in range(slabs):
            send_car(k).wait_send()

        def sent(j, carry):
            s, h = j // 2, j % 2

            when(goes_next(s, h))(lambda: ring_next(s, h).wait_send())
            when(goes_prev(s, h))(lambda: ring_prev(s, h).wait_send())

            return carry

        lax.fori_loop(0, ticks, sent, 0)


def local(nseg, n, energies, hamiltonian, coupling, seed_inverse, lead_green):
    slabs, order, _ = hamiltonian.shape
    width = lead_green.shape[3]
    pad = -(-width // LANES) * LANES
    wide = 2 * pad
    chains = 2 * slabs
    steps = n // 2
    vmem = pl.BlockSpec(memory_space=pltpu.VMEM)
    anywhere = pl.BlockSpec(memory_space=pl.ANY)
    dma = pltpu.SemaphoreType.DMA
    bf16, f32 = jnp.bfloat16, jnp.float32
    turned = pl.pallas_call(
        functools.partial(kernel, nseg, n, width, pad),
        out_shape=jax.ShapeDtypeStruct((2, 1, slabs, width, order), bf16),
        in_specs=[pl.BlockSpec(memory_space=pltpu.SMEM)] + [anywhere] * 3 + [vmem],
        out_specs=vmem,
        scratch_shapes=[
            pltpu.VMEM((slabs, order, order), bf16),
            pltpu.VMEM((slabs, order, order), bf16),
            pltpu.VMEM((2, slabs, order, order), bf16),
            pltpu.VMEM((slabs, order, order), bf16),
            pltpu.VMEM((n, 2, 2 * width, order // 2), bf16),
            pltpu.VMEM((n, 2 * width, chains * wide), bf16),
            pltpu.VMEM((chains, order, wide), bf16),
            pltpu.VMEM((chains, slabs, order, wide), bf16),
            pltpu.VMEM((chains, slabs, order, wide), f32),
            pltpu.VMEM((2, order // 2, chains * wide), f32),
            pltpu.VMEM((chains, order, wide), bf16),
            pltpu.VMEM((2, 2 * width, order // 2), bf16),
            pltpu.VMEM((2, slabs, order, order), bf16),
            pltpu.VMEM((chains, order, wide), f32),
            dma((4, slabs)),
            dma((slabs,)), dma((slabs,)), dma((slabs,)), dma((slabs,)),
            dma((2,)), dma((2,)),
            dma((steps, 2)), dma((steps, 2)), dma((steps, 2)), dma((steps, 2)),
        ],
        compiler_params=pltpu.CompilerParams(
            collective_id=0, has_side_effects=True, vmem_limit_bytes=60 * 2**20
        ),
    )(energies, hamiltonian, coupling, seed_inverse, jnp.swapaxes(lead_green, 2, 3))
    return jnp.swapaxes(turned, 3, 4)


def solution(mesh):
    in_specs = (
        P(),
        P("seg", None, None),
        P("seg", None, None),
        P(None, None, "seg", None, None),
        P(None, None, None, "tr"),
    )
    out_specs = P(None, None, "seg", None, "tr")
    body = functools.partial(local, mesh.shape["seg"], mesh.shape["tr"])
    return jax.shard_map(body, mesh=mesh, in_specs=in_specs, out_specs=out_specs, check_vma=False)
```
